32 devices in a mesh: seq: 16 (over z, y, core), wsh: 2 (over x).
Axes of the slice: x: 2, y: 2, z: 4, core: 2. Of those that a mesh axis runs over, the one named last changes fastest.
Arguments:
- hidden: bfloat16 [8, 1024, 2048], P('wsh', 'seq'), may hold values from -6 to 6
- cotangent: bfloat16 [8, 1024, 2048], P('wsh', 'seq'), may hold values from -6 to 6
- norm_gain: float32 [2048], replicated, may hold values from 0.1 to 1.9
- in_proj: bfloat16 [2048, 8512], P('wsh'), may hold values from -0.088388348 to 0.088388348
- conv_weight: float32 [4, 4352], replicated, may hold values from -3 to 3
- conv_bias: float32 [4352], replicated, may hold values from -1.5 to 1.5
- dt_bias: float32 [64], replicated, may hold values from -1.5 to 0.5
- a_log: float32 [64], replicated, may hold values from -12 to -3.4
- d_skip: float32 [64], replicated, may hold values from 0.5 to 1.5
- gate_gain: float32 [4096], replicated, may hold values from 0.1 to 1.9
- out_proj: bfloat16 [4096, 2048], P('wsh'), may hold values from -0.09375 to 0.09375
Outputs:
- block_out: bfloat16 [8, 1024, 2048], P('wsh', 'seq')
- hidden_grad: float32 [8, 1024, 2048], P('wsh', 'seq')
- norm_gain_grad: float32 [2048], replicated
- in_proj_grad: float32 [2048, 8512], P(('seq', 'wsh'))
- conv_weight_grad: float32 [4, 4352], replicated
- conv_bias_grad: float32 [4352], replicated
- dt_bias_grad: float32 [64], replicated
- a_log_grad: float32 [64], replicated
- d_skip_grad: float32 [64], replicated
- gate_gain_grad: float32 [4096], replicated
- out_proj_grad: float32 [4096, 2048], P(('seq', 'wsh'))
The draws below stay inside these ranges and needn't reach their ends.
All inputs are finite; a program needn't handle non-finite values.
Results may differ from the reference program's by a relative error of at most 0.02.
The reference program's roundings to bfloat16 on the way count: a program that leaves them out, or rounds other values in their place, can miss the bound.
Values may be sent and summed in bfloat16 or wider, within the bound.
No kernel may reach another device: no remote copies, remote signals or barrier semaphores. Data moves between devices by JAX's collectives and lax.ppermute only.
A program may use at most 384 MiB of HBM per device.

```python
import math
import jax
import jax.numpy as jnp
from jax import lax

D = 2048
STATE = 128
HEADS = 64
KERNEL = 4
SPAN = 256
INNER = 4096
PROJ = 8512
CONVDIM = 4352
LEN = 1024
SEQS = 8


def draw_in_proj(key, part):
    key = jax.random.fold_in(key, 11)
    columns = jnp.arange(PROJ)
    column_scale = jnp.where((columns >= 2 * INNER) & (columns < 2 * INNER + 2 * STATE), 0.25, 1.0)
    values = jnp.clip(jax.random.normal(key, (D, PROJ), jnp.float32), -4.0, 4.0)
    return (values * column_scale[None, :] * D ** (-0.5)).astype(jnp.bfloat16)


def draw_a_log(key, part):
    key = jax.random.fold_in(key, 23)
    lower = math.log(0.5 / LEN)
    upper = math.log(1.0 / 30.0)
    return jax.random.uniform(key, (HEADS,), jnp.float32, lower, upper)


def shard_levels(own_key, extent, cuts, low, high):
    loudness = 1.0
    for axis_at, blocks in cuts:
        heights = jax.random.uniform(jax.random.fold_in(jax.random.fold_in(own_key, 6), axis_at), (blocks,), jnp.float32, low / len(cuts), high / len(cuts))
        loudness = loudness * jnp.repeat(jnp.exp(heights), extent[axis_at] // blocks).reshape((-1,) + (1,) * (len(extent) - 1 - axis_at))
    return loudness


def bell_draw(stream_key, shape, width, bound, pieces=(), kind=jnp.bfloat16):
    entries = width * jax.random.normal(stream_key, shape, jnp.float32)
    if pieces:
        entries = entries * shard_levels(stream_key, shape, pieces, -0.22, 0.18)
    return jnp.clip(entries, -bound, bound).astype(kind)


def setup_inputs(seed: int = 0) -> dict:
    key_list = jax.random.split(jax.random.key(seed), 12)
    hidden = bell_draw(key_list[0], (SEQS, LEN, D), 1.0, 6.0, ((0, 2), (1, 16)))
    cotangent = bell_draw(key_list[1], (SEQS, LEN, D), 1.0, 6.0, ((0, 2), (1, 16)))
    norm_gain = jnp.clip(1.0 + 0.18 * jax.random.normal(key_list[2], (D,), jnp.float32), 0.1, 1.9)
    in_proj = draw_in_proj(jax.random.fold_in(key_list[11], 71), 0)
    conv_weight = bell_draw(key_list[4], (KERNEL, CONVDIM), KERNEL ** -0.5, 3.0, (), jnp.float32)
    conv_bias = bell_draw(key_list[5], (CONVDIM,), 0.3, 1.5, (), jnp.float32)
    dt_bias = jnp.clip(jax.random.uniform(key_list[6], (HEADS,), jnp.float32, -1.5, 0.5), -1.5, 0.5)
    a_log = draw_a_log(jax.random.fold_in(key_list[11], 71), 0)
    d_skip = jnp.clip(jax.random.uniform(key_list[8], (HEADS,), jnp.float32, 0.5, 1.5), 0.5, 1.5)
    gate_gain = jnp.clip(1.0 + 0.18 * jax.random.normal(key_list[9], (INNER,), jnp.float32), 0.1, 1.9)
    out_proj = bell_draw(key_list[10], (INNER, D), INNER ** -0.5, 0.09375, ((0, 2),))
    return {"hidden": hidden, "cotangent": cotangent, "norm_gain": norm_gain, "in_proj": in_proj, "conv_weight": conv_weight, "conv_bias": conv_bias, "dt_bias": dt_bias, "a_log": a_log, "d_skip": d_skip, "gate_gain": gate_gain, "out_proj": out_proj}


EPS = 1e-05
HIGH = lax.Precision.HIGHEST

@jax.custom_vjp
def low(v):
    return lax.optimization_barrier(v.astype(jnp.bfloat16)).astype(jnp.float32)

@jax.custom_vjp
def low_back(v):
    return v

def low_keep(v):
    return (low(v), None)

def low_pass(kept, grad):
    return (grad,)

def back_keep(v):
    return (v, None)

def back_low(kept, grad):
    return (low(grad),)
low.defvjp(low_keep, low_pass)
low_back.defvjp(back_keep, back_low)

def rms_norm(values, scale_vec):
    return values * lax.rsqrt(lax.optimization_barrier(jnp.mean(values * values, axis=-1, keepdims=True)) + EPS) * scale_vec

def gated_norm(mixed, gate_part, scale_vec):
    return rms_norm(mixed * jax.nn.silu(gate_part), scale_vec)

def causal_conv(signal, weight, bias_vec):
    tap_count = weight.shape[0]
    length = signal.shape[0]
    padded = jnp.concatenate([jnp.zeros((tap_count - 1, signal.shape[1]), jnp.float32), signal], 0)
    running = bias_vec[None, :] + padded[0:length] * weight[0]
    for offset in range(1, tap_count):
        running = running + padded[offset:offset + length] * weight[offset]
    return running

def span_step(carry, block):
    state, neg_rate = carry
    x_block, step_block, b_block, c_block = block
    cums = jnp.cumsum(step_block * neg_rate[None, :], axis=0)
    cums_head = cums.T
    scores = jnp.dot(c_block, b_block.T, precision=HIGH)
    rows = lax.broadcasted_iota(jnp.int32, (SPAN, SPAN), 0)
    cols = lax.broadcasted_iota(jnp.int32, (SPAN, SPAN), 1)
    causal = (rows >= cols)[None, :, :]
    spread = jnp.where(causal, cums_head[:, :, None] - cums_head[:, None, :], 0.0)
    decay = jnp.where(causal, jnp.exp(spread), 0.0)
    weights = decay * scores[None, :, :] * step_block.T[:, None, :]
    inner = jnp.einsum('hij,jhp->ihp', weights, x_block, precision=HIGH)
    carried = jnp.einsum('in,hnp->ihp', c_block, state, precision=HIGH) * jnp.exp(cums)[:, :, None]
    tail = jnp.exp(cums[-1][None, :] - cums) * step_block
    fresh = jnp.einsum('jh,jn,jhp->hnp', tail, b_block, x_block, precision=HIGH)
    state = state * jnp.exp(cums[-1])[:, None, None] + fresh
    return ((state, neg_rate), inner + carried)

def scan_spans(x_heads, steps, bmat, cmat, neg_rate):
    length, head_count, head_width = x_heads.shape
    count = length // SPAN
    blocks = (x_heads.reshape(count, SPAN, head_count, head_width), steps.reshape(count, SPAN, head_count), bmat.reshape(count, SPAN, bmat.shape[1]), cmat.reshape(count, SPAN, cmat.shape[1]))
    start_state = jnp.zeros((head_count, bmat.shape[1], head_width), jnp.float32)
    carry, outputs = lax.scan(jax.checkpoint(span_step), (start_state, neg_rate), blocks)
    return outputs.reshape(length, head_count, head_width)

def local_mixer(x_in, dt_in, bc_in, conv_x, bias_x, conv_bc, bias_bc, dt_shift, log_rate, skip):
    length = x_in.shape[0]
    head_count = dt_in.shape[1]
    x_act = jax.nn.silu(causal_conv(x_in, conv_x, bias_x))
    bc_act = jax.nn.silu(causal_conv(bc_in, conv_bc, bias_bc))
    steps = jax.nn.softplus(dt_in + dt_shift[None, :])
    x_heads = x_act.reshape(length, head_count, x_act.shape[1] // head_count)
    state_size = bc_act.shape[1] // 2
    outputs = scan_spans(x_heads, steps, bc_act[:, :state_size], bc_act[:, state_size:], -jnp.exp(log_rate))
    outputs = outputs + skip[None, :, None] * x_heads
    return outputs.reshape(length, x_act.shape[1])

def reference(hidden, cotangent, norm_gain, in_proj, conv_weight, conv_bias, dt_bias, a_log, d_skip, gate_gain, out_proj):

    def forward(tokens, ngain, w_in, cweight, cbias, dshift, lograte, skip, ggain, w_out):

        def one_sequence(sequence):
            normed = low(rms_norm(sequence, ngain))
            proj = low(low_back(jnp.dot(normed, w_in, precision=HIGH)))
            gate_part = proj[:, :INNER]
            x_in = proj[:, INNER:2 * INNER]
            bc_in = proj[:, 2 * INNER:2 * INNER + 2 * STATE]
            dt_in = proj[:, 2 * INNER + 2 * STATE:]
            mixed = local_mixer(x_in, dt_in, bc_in, cweight[:, :INNER], cbias[:INNER], cweight[:, INNER:], cbias[INNER:], dshift, lograte, skip)
            mixed = low(low_back(mixed))
            gated = low(gated_norm(mixed, gate_part, ggain))
            return sequence + jnp.dot(gated, w_out, precision=HIGH)
        return lax.map(one_sequence, tokens)
    inputs = (hidden.astype(jnp.float32), norm_gain, in_proj.astype(jnp.float32), conv_weight, conv_bias, dt_bias, a_log, d_skip, gate_gain, out_proj.astype(jnp.float32))
    result, pullback = jax.vjp(forward, *inputs)
    grads = pullback(cotangent.astype(jnp.float32))
    return (result.astype(jnp.bfloat16), grads[0], grads[1], grads[2], grads[3], grads[4], grads[5], grads[6], grads[7], grads[8], grads[9])
```

```python
import functools
import jax
import jax.numpy as jnp
from jax import lax
from jax.experimental import pallas as pl
from jax.experimental.pallas import tpu as pltpu
from jax.sharding import Mesh
from jax.sharding import PartitionSpec as P

STATE = 128
HEADDIM = 64
SPAN = 256
INNER = 4096
EPS = 1e-05
HIGH = lax.Precision.HIGHEST
NEG = -1e30
F32 = jnp.float32
BF16 = jnp.bfloat16


def dot_plain(left, right, precision=None):
    return lax.dot_general(
        left, right, (((1,), (0,)), ((), ())), preferred_element_type=F32, precision=precision
    )


def dot_lanes(left, right):
    return lax.dot_general(left, right, (((1,), (1,)), ((), ())), preferred_element_type=F32)


def dot_rows(left, right):
    return lax.dot_general(left, right, (((0,), (0,)), ((), ())), preferred_element_type=F32)


def softplus(values):
    return jnp.maximum(values, 0.0) + jnp.log1p(jnp.exp(-jnp.abs(values)))


def sigmoid(values):
    return 1.0 / (1.0 + jnp.exp(-values))


def head_rows(raw_steps, shift, neg_rate):
    span, heads = raw_steps.shape
    wide = jnp.concatenate([raw_steps, jnp.zeros((span, 128 - heads), F32)], 1)
    raw = wide.T[:heads] + shift
    step = softplus(raw)
    order = lax.broadcasted_iota(jnp.int32, (span, span), 0)
    until = lax.broadcasted_iota(jnp.int32, (span, span), 1)
    upper = jnp.where(order <= until, 1.0, 0.0)
    cum = dot_plain(step * neg_rate, upper, HIGH)
    last = cum[:, span - 1 :]
    return raw, step, cum, jnp.exp(cum), jnp.exp(last - cum)


def as_columns(rows):
    count, span = rows.shape
    return jnp.concatenate([rows, jnp.zeros((128 - count, span), F32)], 0).T


def spread_lanes(columns, start, heads):
    span = columns.shape[0]
    low = lax.broadcasted_iota(jnp.int32, (span, 2 * HEADDIM), 1) < HEADDIM
    pieces = []
    for pair in range(heads // 2):
        at = start + 2 * pair
        pieces.append(jnp.where(low, columns[:, at : at + 1], columns[:, at + 1 : at + 2]))
    return jnp.concatenate(pieces, 1)


def pair_halves(values, pair):
    slab = values[:, 2 * HEADDIM * pair : 2 * HEADDIM * (pair + 1)]
    low = lax.broadcasted_iota(jnp.int32, slab.shape, 1) < HEADDIM
    zero = jnp.zeros_like(slab)
    return slab, (jnp.where(low, slab, zero), jnp.where(low, zero, slab))


def convolve(window, taps, offset, span):
    running = None
    for k in range(taps.shape[0]):
        term = window[pl.ds(offset(k), span), :] * taps[k : k + 1, :]
        running = term if running is None else running + term
    return running


def scan_forward_body(
    heads,
    raw_ref,
    taps_ref,
    bias_ref,
    shift_ref,
    rate_ref,
    skip_ref,
    mixed_ref,
    start_ref,
    edge_ref,
    state,
    window,
):
    span = raw_ref.shape[0]
    inner = heads * HEADDIM
    wide = inner + 2 * STATE
    first = pl.program_id(1) == 0

    @pl.when(first)
    def _():
        state[...] = jnp.zeros_like(state)
        window[0:8, :] = jnp.zeros((8, wide), F32)

    @pl.when(jnp.logical_not(first))
    def _():
        window[0:8, :] = window[span : span + 8, :]

    edge_ref[...] = window[0:8, :]
    window[8 : 8 + span, :] = raw_ref[:, :wide].astype(F32)
    conv = convolve(window, taps_ref[...], lambda k: 5 + k, span) + bias_ref[...]
    act = conv * sigmoid(conv)
    x_act = act[:, :inner]
    b_low = act[:, inner : inner + STATE].astype(BF16)
    c_act = act[:, inner + STATE :]
    c_low = c_act.astype(BF16)
    c_both = jnp.concatenate([c_low, (c_act - c_low.astype(F32)).astype(BF16)], 1)
    raw, step, cum, grown, tail = head_rows(
        raw_ref[:, wide:].astype(F32), shift_ref[...], -jnp.exp(rate_ref[...])
    )
    columns = as_columns(jnp.concatenate([cum, step, grown, tail], 0))
    step_wide = spread_lanes(columns, heads, heads)
    grown_wide = spread_lanes(columns, 2 * heads, heads)
    tail_wide = spread_lanes(columns, 3 * heads, heads)
    stepped = x_act * step_wide
    stepped_low = stepped.astype(BF16)
    held = state[...]
    start_ref[...] = held
    held_low = held.astype(BF16)
    scores = dot_lanes(c_both, jnp.concatenate([b_low, b_low], 1))
    carried = dot_plain(c_both, jnp.concatenate([held_low, held_low], 0)) * grown_wide
    carried = carried + skip_ref[...] * x_act
    rows = lax.broadcasted_iota(jnp.int32, (span, span), 0)
    cols = lax.broadcasted_iota(jnp.int32, (span, span), 1)
    causal = rows >= cols
    for pair in range(heads // 2):
        _, halves = pair_halves(stepped_low, pair)
        total = carried[:, 2 * HEADDIM * pair : 2 * HEADDIM * (pair + 1)]
        for half in range(2):
            head = 2 * pair + half
            spread = columns[:, head : head + 1] - cum[head : head + 1, :]
            weights = jnp.exp(jnp.where(causal, spread, NEG)) * scores
            total = total + dot_plain(weights.astype(BF16), halves[half])
        mixed_ref[:, 2 * HEADDIM * pair : 2 * HEADDIM * (pair + 1)] = total.astype(BF16)
    fresh = dot_rows(b_low, (stepped * tail_wide).astype(BF16))
    state[...] = held * grown_wide[span - 1 : span, :] + fresh


def scan_forward(raw, at, taps, bias, shift, log_rate, skip_wide):
    _, length, width = raw.shape
    seqs = 1
    heads = shift.shape[0]
    inner = heads * HEADDIM
    wide = inner + 2 * STATE
    spans = length // SPAN
    whole = lambda shape: pl.BlockSpec(shape, lambda s, i: (0,) * len(shape))
    return pl.pallas_call(
        functools.partial(scan_forward_body, heads),
        grid=(seqs, spans),
        in_specs=[
            pl.BlockSpec((None, SPAN, width), lambda s, i: (at, i, 0)),
            whole(taps.shape),
            whole(bias.shape),
            whole(shift.shape),
            whole(log_rate.shape),
            whole(skip_wide.shape),
        ],
        out_specs=[
            pl.BlockSpec((None, SPAN, inner), lambda s, i: (s, i, 0)),
            pl.BlockSpec((None, None, STATE, inner), lambda s, i: (s, i, 0, 0)),
            pl.BlockSpec((None, None, 8, wide), lambda s, i: (s, i, 0, 0)),
        ],
        out_shape=[
            jax.ShapeDtypeStruct((seqs, length, inner), BF16),
            jax.ShapeDtypeStruct((seqs, spans, STATE, inner), F32),
            jax.ShapeDtypeStruct((seqs, spans, 8, wide), F32),
        ],
        scratch_shapes=[pltpu.VMEM((STATE, inner), F32), pltpu.VMEM((SPAN + 8, wide), F32)],
        compiler_params=kernel_params(),
        cost_estimate=light_cost(length),
        name="scan_forward",
    )(raw, taps, bias, shift, log_rate, skip_wide)


def scan_backward_body(
    heads,
    raw_ref,
    down_ref,
    start_ref,
    edge_ref,
    taps_ref,
    bias_ref,
    shift_ref,
    rate_ref,
    skip_ref,
    draw_ref,
    dtaps_ref,
    dskip_ref,
    dhead_ref,
    dstate,
    window,
    ahead,
):
    span = raw_ref.shape[0]
    inner = heads * HEADDIM
    wide = inner + 2 * STATE
    step_at = pl.program_id(1)

    @pl.when((pl.program_id(0) == 0) & (step_at == 0))
    def _():
        dtaps_ref[...] = jnp.zeros_like(dtaps_ref)
        dskip_ref[...] = jnp.zeros_like(dskip_ref)
        dhead_ref[...] = jnp.zeros_like(dhead_ref)

    @pl.when(step_at == 0)
    def _():
        dstate[...] = jnp.zeros_like(dstate)
        ahead[span : span + 8, :] = jnp.zeros((8, wide), F32)

    @pl.when(step_at != 0)
    def _():
        ahead[span : span + 8, :] = ahead[0:8, :]

    taps = taps_ref[...]
    window[0:8, :] = edge_ref[...]
    window[8 : 8 + span, :] = raw_ref[:, :wide].astype(F32)
    conv = convolve(window, taps, lambda k: 5 + k, span) + bias_ref[...]
    sig = sigmoid(conv)
    act = conv * sig
    x_act = act[:, :inner]
    b_low = act[:, inner : inner + STATE].astype(BF16)
    c_low = act[:, inner + STATE :].astype(BF16)
    neg_rate = -jnp.exp(rate_ref[...])
    raw, step, cum, grown, tail = head_rows(raw_ref[:, wide:].astype(F32), shift_ref[...], neg_rate)
    columns = as_columns(jnp.concatenate([cum, step, grown, tail], 0))
    step_wide = spread_lanes(columns, heads, heads)
    grown_wide = spread_lanes(columns, 2 * heads, heads)
    tail_wide = spread_lanes(columns, 3 * heads, heads)
    stepped = x_act * step_wide
    stepped_low = stepped.astype(BF16)
    down_low = down_ref[...]
    down = down_low.astype(F32)
    held = start_ref[...]
    held_low = held.astype(BF16)
    dheld = dstate[...]
    dheld_low = dheld.astype(BF16)
    scores = dot_lanes(b_low, c_low)
    rows = lax.broadcasted_iota(jnp.int32, (span, span), 0)
    cols = lax.broadcasted_iota(jnp.int32, (span, span), 1)
    causal = cols >= rows
    dscores = jnp.zeros((span, span), F32)
    dstepped_parts = []
    gained = []
    lost = []
    for pair in range(heads // 2):
        _, x_halves = pair_halves(stepped_low, pair)
        down_pair, down_halves = pair_halves(down_low, pair)
        total = jnp.zeros((span, 2 * HEADDIM), F32)
        for half in range(2):
            head = 2 * pair + half
            spread = cum[head : head + 1, :] - columns[:, head : head + 1]
            decay = jnp.exp(jnp.where(causal, spread, NEG))
            weights = decay * scores
            dweights = dot_lanes(x_halves[half], down_pair)
            dscores = dscores + decay * dweights
            both = weights * dweights
            gained.append(jnp.sum(both, axis=0, keepdims=True))
            lost.append(jnp.sum(both, axis=1, keepdims=True))
            total = total + dot_plain(weights.astype(BF16), down_halves[half])
        dstepped_parts.append(total)
    dscores_low = dscores.astype(BF16)
    dtail = dot_plain(b_low, dheld_low) * tail_wide
    dstepped = jnp.concatenate(dstepped_parts, 1) + dtail
    down_grown = (down * grown_wide).astype(BF16)
    d_b = dot_plain(dscores_low, c_low) + dot_lanes((stepped * tail_wide).astype(BF16), dheld_low)
    d_c = dot_rows(dscores_low, b_low) + dot_lanes(down_grown, held_low)
    carried = dot_plain(c_low, held_low) * grown_wide
    member = lax.broadcasted_iota(jnp.int32, (heads, inner), 1) // HEADDIM
    which = lax.broadcasted_iota(jnp.int32, (heads, inner), 0)
    pick = jnp.where(member == which, 1.0, 0.0)
    pick_low = pick.astype(BF16)
    carried_sum = dot_lanes(pick_low, (down * carried).astype(BF16))
    tail_sum = dot_lanes(pick_low, (stepped * dtail).astype(BF16))
    step_sum = dot_lanes(pick_low, (x_act * dstepped).astype(BF16))
    lost_rows = as_columns_back(jnp.concatenate(lost, 1))
    state_sum = jnp.sum(pick * jnp.sum(held * dheld, axis=0, keepdims=True), axis=1, keepdims=True)
    dcum = jnp.concatenate(gained, 0) + carried_sum - lost_rows - tail_sum
    since = jnp.where(rows >= cols, 1.0, 0.0)
    whole_part = jnp.sum(tail_sum, axis=1, keepdims=True) + grown[:, span - 1 :] * state_sum
    dlog = dot_plain(dcum, since, HIGH) + whole_part
    draw_step = (step_sum + neg_rate * dlog) * sigmoid(raw)
    dhead_ref[0] += neg_rate * jnp.sum(step * dlog, axis=1, keepdims=True)
    dhead_ref[1] += jnp.sum(draw_step, axis=1, keepdims=True)
    dskip_ref[...] += jnp.sum(down * x_act, axis=0, keepdims=True)
    d_x = dstepped * step_wide + skip_ref[...] * down
    dconv = jnp.concatenate([d_x, d_b, d_c], 1) * (sig * (1.0 + conv * (1.0 - sig)))
    ahead[0:span, :] = dconv
    draw = convolve(ahead, taps, lambda k: 3 - k, span)
    draw_ref[:, :wide] = draw.astype(BF16)
    draw_ref[:, wide:] = as_columns(draw_step)[:, :heads].astype(BF16)
    for k in range(taps.shape[0]):
        dtaps_ref[k : k + 1, :] += jnp.sum(
            dconv * window[pl.ds(5 + k, span), :], axis=0, keepdims=True
        )
    dtaps_ref[4:5, :] += jnp.sum(dconv, axis=0, keepdims=True)
    dstate[...] = dheld * grown_wide[span - 1 : span, :] + dot_rows(c_low, down_grown)


def as_columns_back(columns):
    span, heads = columns.shape
    return jnp.concatenate([columns, jnp.zeros((span, 128 - heads), F32)], 1).T[:heads]


def scan_backward(raw, at, down, starts, edges, taps, bias, shift, log_rate, skip_wide):
    _, length, width = raw.shape
    seqs = 1
    heads = shift.shape[0]
    inner = heads * HEADDIM
    wide = inner + 2 * STATE
    spans = length // SPAN
    whole = lambda shape: pl.BlockSpec(shape, lambda s, i: (0,) * len(shape))
    turned = lambda s, i: (s, spans - 1 - i, 0)
    return pl.pallas_call(
        functools.partial(scan_backward_body, heads),
        grid=(seqs, spans),
        in_specs=[
            pl.BlockSpec((None, SPAN, width), lambda s, i: (at, spans - 1 - i, 0)),
            pl.BlockSpec((None, SPAN, inner), turned),
            pl.BlockSpec((None, None, STATE, inner), lambda s, i: (s, spans - 1 - i, 0, 0)),
            pl.BlockSpec((None, None, 8, wide), lambda s, i: (s, spans - 1 - i, 0, 0)),
            whole(taps.shape),
            whole(bias.shape),
            whole(shift.shape),
            whole(log_rate.shape),
            whole(skip_wide.shape),
        ],
        out_specs=[
            pl.BlockSpec((None, SPAN, width), turned),
            whole((8, wide)),
            whole((1, inner)),
            whole((2, heads, 1)),
        ],
        out_shape=[
            jax.ShapeDtypeStruct((seqs, length, width), BF16),
            jax.ShapeDtypeStruct((8, wide), F32),
            jax.ShapeDtypeStruct((1, inner), F32),
            jax.ShapeDtypeStruct((2, heads, 1), F32),
        ],
        scratch_shapes=[
            pltpu.VMEM((STATE, inner), F32),
            pltpu.VMEM((SPAN + 8, wide), F32),
            pltpu.VMEM((SPAN + 8, wide), F32),
        ],
        compiler_params=kernel_params(),
        cost_estimate=light_cost(length),
        name="scan_backward",
    )(raw, down, starts, edges, taps, bias, shift, log_rate, skip_wide)


def kernel_params():
    return pltpu.CompilerParams(vmem_limit_bytes=30 * 1024 * 1024)


def light_cost(count):
    return pl.CostEstimate(flops=count, bytes_accessed=count, transcendentals=0)


def project_body(inner, tokens_ref, weight_ref, gate_ref, raw_ref, turned_ref):
    _, _, tokens, model = tokens_ref.shape
    values = tokens_ref[...].reshape(4 * tokens, model)
    put_by_member(gate_ref, dot_lanes(values, weight_ref[:inner, :]))
    put_by_member(raw_ref, dot_lanes(values, weight_ref[inner:, :]))
    for half in range(2):
        pair = jnp.concatenate([tokens_ref[core, half] for core in range(2)], 0)
        turned_ref[half] = pair.T


def project_tokens(values, weight, inner):
    team, _, tokens, model = values.shape
    width = weight.shape[0]

    def natural(size):
        return pl.BlockSpec((2, 2, tokens, size), lambda i: (0, i, 0, 0))

    return pl.pallas_call(
        functools.partial(project_body, inner),
        grid=(team // 2,),
        in_specs=[
            pl.BlockSpec((2, 2, tokens, model), lambda i: (i, 0, 0, 0)),
            pl.BlockSpec((width, model), lambda i: (0, 0)),
        ],
        out_specs=[
            natural(inner),
            natural(width - inner),
            pl.BlockSpec((2, model, 2 * tokens), lambda i: (0, 0, i)),
        ],
        out_shape=[
            jax.ShapeDtypeStruct((2, team, tokens, inner), BF16),
            jax.ShapeDtypeStruct((2, team, tokens, width - inner), BF16),
            jax.ShapeDtypeStruct((2, model, team * tokens), BF16),
        ],
        compiler_params=kernel_params(),
        cost_estimate=light_cost(team),
        name="project_tokens",
    )(values, weight)


def by_member(ref):
    return jnp.concatenate(
        [ref[half, member] for member in range(ref.shape[1]) for half in range(2)], 0
    )


def put_by_member(ref, rows):
    tokens = ref.shape[2]
    for member in range(ref.shape[1]):
        for half in range(2):
            at = (member * 2 + half) * tokens
            ref[half, member] = rows[at : at + tokens].astype(ref.dtype)


def gate_stats_body(grad_ref, weight_ref, mixed_ref, gate_ref, gain_ref, down_ref, sums_ref):
    pair, _, tokens, model = grad_ref.shape
    d_gated = dot_lanes(grad_ref[...].reshape(pair * 2 * tokens, model), weight_ref[...])
    gate = by_member(gate_ref).astype(F32)
    unit = by_member(mixed_ref).astype(F32) * gate * sigmoid(gate)
    put_by_member(down_ref, d_gated)
    square = jnp.sum(unit * unit, axis=1, keepdims=True)
    cross = jnp.sum(d_gated * gain_ref[...] * unit, axis=1, keepdims=True)
    sums_ref[...] = as_columns_back(jnp.concatenate([square, cross], 1))


def gate_stats(grad, weight, mixed, gate, gain):
    team, _, tokens, model = grad.shape
    inner = weight.shape[0]
    pair = 2
    rows = pair * 2 * tokens
    natural = pl.BlockSpec((2, pair, tokens, inner), lambda i: (0, i, 0, 0))
    return pl.pallas_call(
        gate_stats_body,
        grid=(team // pair,),
        in_specs=[
            pl.BlockSpec((pair, 2, tokens, model), lambda i: (i, 0, 0, 0)),
            pl.BlockSpec((inner, model), lambda i: (0, 0)),
            natural,
            natural,
            pl.BlockSpec((1, inner), lambda i: (0, 0)),
        ],
        out_specs=[
            natural,
            pl.BlockSpec((2, rows), lambda i: (0, i)),
        ],
        out_shape=[
            jax.ShapeDtypeStruct((2, team, tokens, inner), F32),
            jax.ShapeDtypeStruct((2, team * 2 * tokens), F32),
        ],
        compiler_params=kernel_params(),
        cost_estimate=light_cost(team),
        name="gate_stats",
    )(grad, weight, mixed, gate, gain)


def put_by_core(own, keep_ref, send_ref, rows):
    tokens = keep_ref.shape[1]
    first, second = rows[: 2 * tokens], rows[2 * tokens :]
    kept = jnp.where(own == 0, first, second)
    sent = jnp.where(own == 0, second, first)
    for half in range(2):
        keep_ref[half] = kept[half * tokens : (half + 1) * tokens].astype(BF16)
        send_ref[half] = sent[half * tokens : (half + 1) * tokens].astype(BF16)


def gate_back_body(
    table_ref,
    mixed_ref,
    gate_ref,
    down_ref,
    sums_ref,
    gain_ref,
    weight_ref,
    turned_ref,
    d_mixed_ref,
    d_gate_ref,
    keep_ref,
    send_ref,
    d_gain_ref,
):
    @pl.when(pl.program_id(0) == 0)
    def _():
        d_gain_ref[...] = jnp.zeros_like(d_gain_ref)

    columns = as_columns(sums_ref[...])
    gain = gain_ref[...]
    scale = lax.rsqrt(columns[:, 0:1] / INNER + EPS)
    pull = columns[:, 1:2] * (scale * scale * scale / INNER)
    mixed = by_member(mixed_ref).astype(F32)
    gate = by_member(gate_ref).astype(F32)
    down = by_member(down_ref)
    sig = sigmoid(gate)
    act = gate * sig
    unit = mixed * act
    scaled = unit * scale
    gated_wide = scaled * gain
    turned_ref[...] = gated_wide.T.astype(BF16)
    out = dot_plain(gated_wide.astype(BF16), weight_ref[...])
    put_by_core(table_ref[0], keep_ref, send_ref, out)
    d_unit = down * gain * scale - unit * pull
    put_by_member(d_mixed_ref, d_unit * act)
    put_by_member(d_gate_ref, d_unit * mixed * (sig * (1.0 + gate * (1.0 - sig))))
    d_gain_ref[...] += jnp.sum(down * scaled, axis=0, keepdims=True)


def gate_back(table, mixed, gate, down, sums, gain, weight):
    _, team, tokens, inner = down.shape
    model = weight.shape[1]
    chips = team // 2
    rows = 4 * tokens
    natural = pl.BlockSpec((2, 2, tokens, inner), lambda i, t: (0, t[1 + i], 0, 0))
    block = pl.BlockSpec((None, 2, tokens, model), lambda i, t: (i, 0, 0, 0))
    one = pl.BlockSpec((1, inner), lambda i, t: (0, 0))
    return pl.pallas_call(
        gate_back_body,
        grid_spec=pltpu.PrefetchScalarGridSpec(
            num_scalar_prefetch=1,
            grid=(chips,),
            in_specs=[
                natural,
                natural,
                natural,
                pl.BlockSpec((2, rows), lambda i, t: (0, t[1 + i])),
                one,
                pl.BlockSpec((inner, model), lambda i, t: (0, 0)),
            ],
            out_specs=[
                pl.BlockSpec((inner, rows), lambda i, t: (0, t[1 + i])),
                natural,
                natural,
                block,
                block,
                one,
            ],
        ),
        out_shape=[
            jax.ShapeDtypeStruct((inner, team * 2 * tokens), BF16),
            jax.ShapeDtypeStruct((2, team, tokens, inner), BF16),
            jax.ShapeDtypeStruct((2, team, tokens, inner), BF16),
            jax.ShapeDtypeStruct((chips, 2, tokens, model), BF16),
            jax.ShapeDtypeStruct((chips, 2, tokens, model), BF16),
            jax.ShapeDtypeStruct((1, inner), F32),
        ],
        compiler_params=kernel_params(),
        cost_estimate=light_cost(team),
        name="gate_back",
    )(table, mixed, gate, down, sums, gain, weight)


def row_grad_body(pairs, cols, has_base, *refs):
    out_ref = refs[-1]
    total = None
    for k in range(pairs):
        left_ref = refs[2 * k]
        right_ref = refs[2 * k + 1]
        count, _, depth = left_ref.shape
        for part in range(count):
            right = right_ref[part * depth : (part + 1) * depth, :]
            if cols is not None:
                right = right[:, cols[0] : cols[1]]
            term = dot_plain(left_ref[part], right)
            total = term if total is None else total + term
    if has_base:
        base = refs[2 * pairs][...]
        if cols is not None:
            base = base[:, cols[0] : cols[1]]
        total = total + base
    out_ref[...] = total.astype(out_ref.dtype)


def row_grad(operands, kind, cols=None, base=None):
    rows = operands[0][0].shape[1]
    width = operands[0][1].shape[1]
    got = width if cols is None else cols[1] - cols[0]
    tile = min(512, rows)
    if got > 1024:
        tile = min(256, rows)
    specs, args = [], []
    for left, right in operands:
        specs.append(pl.BlockSpec((left.shape[0], tile, left.shape[2]), lambda i: (0, i, 0)))
        specs.append(pl.BlockSpec(right.shape, lambda i: (0, 0)))
        args += [left, right]
    if base is not None:
        specs.append(pl.BlockSpec((tile, width), lambda i: (i, 0)))
        args.append(base)
    return pl.pallas_call(
        functools.partial(row_grad_body, len(operands), cols, base is not None),
        grid=(rows // tile,),
        in_specs=specs,
        out_specs=pl.BlockSpec((tile, got), lambda i: (i, 0)),
        out_shape=jax.ShapeDtypeStruct((rows, got), kind),
        compiler_params=kernel_params(),
        cost_estimate=light_cost(rows),
        name="row_grad",
    )(*args)


def norm_part_body(
    table_ref, d_gate_ref, d_raw_ref, normed_ref, weight_ref, keep_ref, send_ref, gain_ref
):
    @pl.when(pl.program_id(0) == 0)
    def _():
        gain_ref[...] = jnp.zeros_like(gain_ref)

    inner = d_gate_ref.shape[-1]
    tokens = keep_ref.shape[1]
    model = keep_ref.shape[2]
    part = dot_plain(by_member(d_gate_ref), weight_ref[:inner, :])
    part = part + dot_plain(by_member(d_raw_ref), weight_ref[inner:, :])
    normed = normed_ref[...].reshape(4 * tokens, model).astype(F32)
    gain_ref[...] += jnp.sum(part * normed, axis=0, keepdims=True)
    put_by_core(table_ref[0], keep_ref, send_ref, part)


def norm_part(table, d_gate, d_raw, normed, weight):
    _, team, tokens, inner = d_gate.shape
    chips = team // 2
    width = d_raw.shape[-1]
    model = weight.shape[1]

    def natural(size):
        return pl.BlockSpec((2, 2, tokens, size), lambda i, t: (0, t[1 + i], 0, 0))

    block = pl.BlockSpec((None, 2, tokens, model), lambda i, t: (i, 0, 0, 0))
    return pl.pallas_call(
        norm_part_body,
        grid_spec=pltpu.PrefetchScalarGridSpec(
            num_scalar_prefetch=1,
            grid=(chips,),
            in_specs=[
                natural(inner),
                natural(width),
                pl.BlockSpec((2, 2, tokens, model), lambda i, t: (t[1 + i], 0, 0, 0)),
                pl.BlockSpec((inner + width, model), lambda i, t: (0, 0)),
            ],
            out_specs=[block, block, pl.BlockSpec((1, model), lambda i, t: (0, 0))],
        ),
        out_shape=[
            jax.ShapeDtypeStruct((chips, 2, tokens, model), BF16),
            jax.ShapeDtypeStruct((chips, 2, tokens, model), BF16),
            jax.ShapeDtypeStruct((1, model), F32),
        ],
        compiler_params=kernel_params(),
        cost_estimate=light_cost(chips),
        name="norm_part",
    )(table, d_gate, d_raw, normed, weight)


TEAM = ("chip", "core")
ALL = ("half", "chip", "core")
EVERY = ALL + ("wsh",)


def after(values, *done):
    leaves, tree = jax.tree.flatten(values)
    others = jax.tree.leaves(done)
    out = lax.optimization_barrier(tuple(leaves) + tuple(others))
    return jax.tree.unflatten(tree, out[: len(leaves)])


def join(*values):
    leaves, tree = jax.tree.flatten(values)
    return jax.tree.unflatten(tree, lax.optimization_barrier(tuple(leaves)))


class Layout:
    def __init__(self):
        self.chips = lax.axis_size("chip")
        self.wsh = lax.axis_size("wsh")
        self.team = 2 * self.chips
        self.parts = 2 * self.team
        self.half = lax.axis_index("half")
        self.chip = lax.axis_index("chip")
        self.core = lax.axis_index("core")
        self.wplace = lax.axis_index("wsh")
        self.member = self.chip * 2 + self.core
        self.block = self.core * self.chips + self.chip

    def other_core(self, values):
        return lax.ppermute(values, "core", [(0, 1), (1, 0)])

    def other_half(self, values):
        return lax.ppermute(values, "half", [(0, 1), (1, 0)])

    def chip_flip(self, values, bits):
        return lax.ppermute(values, "chip", [(i, i ^ bits) for i in range(self.chips)])

    def wsh_shift(self, values, shift):
        size = self.wsh
        return lax.ppermute(values, "wsh", [(i, (i + shift) % size) for i in range(size)])


def pick(values, at, axis):
    return lax.dynamic_index_in_dim(values, at, axis, keepdims=False)


def split_halves(own, lay):
    count = own.shape[0] // 2
    keep = lax.dynamic_slice_in_dim(own, lay.half * count, count, 0)
    away = lax.dynamic_slice_in_dim(own, (1 - lay.half) * count, count, 0)
    return keep, away


def team_gather(keep, came, lay):
    pair = jnp.where(lay.half == 0, jnp.stack([keep, came]), jnp.stack([came, keep]))
    return lax.all_gather(pair, TEAM, axis=0)


def both_halves(mine, other, lay):
    first = jnp.where(lay.half == 0, mine, other)
    second = jnp.where(lay.half == 0, other, mine)
    return jnp.concatenate([first, second], 0)


def core_sum(keep, came):
    return (keep.astype(F32) + came.astype(F32)).astype(BF16)


def chip_parts(added, lay):
    return [added[0]] + [lay.chip_flip(added[bits], bits) for bits in range(1, lay.chips)]


def chip_sum(parts, lay):
    own = add_all([part.astype(F32) for part in parts]).astype(BF16)
    return pick(own, lay.half, 0), pick(own, 1 - lay.half, 0)


def columns_in_place(local, came, lay):
    wide = local.shape[1]
    full = jnp.zeros((local.shape[0], lay.wsh * wide), local.dtype)
    full = lax.dynamic_update_slice_in_dim(full, local, lay.wplace * wide, 1)
    for start, pieces in came:
        for shift, piece in enumerate(pieces):
            at = ((lay.wplace - shift - 1) % lay.wsh) * wide
            full = lax.dynamic_update_slice(full, piece, (start, at))
    return full


def team_parts(values, lay):
    values = values + lay.other_core(values)
    return [values] + [lay.chip_flip(values, bits) for bits in range(1, lay.chips)]


def add_all(parts):
    while len(parts) > 1:
        parts = [parts[k] + parts[k + 1] for k in range(0, len(parts), 2)]
    return parts[0]


class Order:
    def __init__(self):
        self.last = ()

    def __call__(self, step, first, *rest):
        first = after(first, self.last)
        out = step(first, *rest)
        self.last = (jax.tree.leaves(out)[0],)
        return out


def shards(
    hidden,
    cotangent,
    norm_gain,
    in_proj,
    conv_weight,
    conv_bias,
    dt_bias,
    a_log,
    d_skip,
    gate_gain,
    out_proj,
):
    lay = Layout()
    seqs, tokens, model = hidden.shape
    count = seqs // 2
    length = tokens * lay.parts
    inner = INNER // lay.team
    heads = inner // HEADDIM
    block = lay.block
    steps_at = 2 * INNER + 2 * STATE

    def columns(values, start, width, axis=1):
        return lax.dynamic_slice_in_dim(values, start, width, axis)

    hidden_wide = hidden.astype(F32)
    norm_scale = lax.rsqrt(jnp.mean(hidden_wide * hidden_wide, axis=-1, keepdims=True) + EPS)
    normed = (hidden_wide * norm_scale * norm_gain).astype(BF16)

    turned = in_proj.T
    local = jnp.concatenate(
        [
            columns(turned, block * inner, inner, 0),
            columns(turned, INNER + block * inner, inner, 0),
            turned[2 * INNER : steps_at],
            columns(turned, steps_at + block * heads, heads, 0),
        ],
        0,
    )

    def to_wsh(values):
        return [lay.wsh_shift(values, shift) for shift in range(1, lay.wsh)]

    cut = (inner // 128 + 1) * 128
    keep, away = split_halves(normed, lay)
    came_first, came = join(to_wsh(local[:cut]), lay.other_half(away))
    keep_grad, away_grad = split_halves(cotangent, lay)
    normeds = [team_gather(keep[0], came[0], lay)]
    came_last, came_grad = join(
        to_wsh(after(local[cut:], came_first)), lay.other_half(after(away_grad, came))
    )
    weight = columns_in_place(local, [(0, came_first), (cut, came_last)], lay)
    rows_held = INNER // lay.wsh
    owner = (block * inner) // rows_held
    at_row = jnp.where(owner == lay.wplace, block * inner - owner * rows_held, 0)
    rows_here = after(columns(out_proj, at_row, inner, 0), came_last)
    w_out = jnp.where(owner == lay.wplace, rows_here, jnp.zeros_like(rows_here))
    for shift in range(1, lay.wsh):
        pairs = []
        for place in range(lay.team):
            head_block = (place % 2) * lay.chips + place // 2
            holder = (head_block * inner) // rows_held
            source = place * lay.wsh + holder
            pairs.append((source, place * lay.wsh + (holder + shift) % lay.wsh))
        w_out = w_out + lax.ppermute(rows_here, TEAM + ("wsh",), pairs)
    keep_grad = after(keep_grad, came_last)
    grads = [team_gather(keep_grad[0], came_grad[0], lay)]
    for s in range(1, count):
        normeds.append(team_gather(*after((keep[s], came[s]), came_last), lay))
        grads.append(team_gather(keep_grad[s], came_grad[s], lay))

    taps = jnp.concatenate(
        [columns(conv_weight, block * inner, inner), conv_weight[:, INNER:]], 1
    )
    bias = jnp.concatenate([columns(conv_bias, block * inner, inner, 0), conv_bias[INNER:]], 0)
    shift_own = columns(dt_bias, block * heads, heads, 0)[:, None]
    rate_own = columns(a_log, block * heads, heads, 0)[:, None]
    skip_own = jnp.repeat(columns(d_skip, block * heads, heads, 0), HEADDIM)[None]
    gain_own = columns(gate_gain, block * inner, inner, 0)[None]
    params = (taps, bias[None], shift_own, rate_own, skip_own)
    table = jnp.stack([lay.core] + [lay.chip ^ d for d in range(lay.chips)]).astype(jnp.int32)

    kernel = conv_weight.shape[0]
    shapes = [norm_gain.shape, conv_weight.shape, conv_bias.shape]
    shapes += [dt_bias.shape, a_log.shape, d_skip.shape, gate_gain.shape]

    def placed(values, width):
        full = jnp.zeros(values.shape[:-1] + (width,), F32)
        return lax.dynamic_update_slice_in_dim(
            full, values, block * values.shape[-1], values.ndim - 1
        )

    def pack_small(norm_gain1):
        d_taps, d_skip_wide, d_head = jax.tree.map(lambda *v: sum(v[1:], v[0]), *small_scan)
        small = [
            (norm_gain0 + norm_gain1)[0] / norm_gain,
            jnp.concatenate([placed(d_taps[:kernel, :inner], INNER), d_taps[:kernel, inner:]], 1),
            jnp.concatenate([placed(d_taps[kernel, :inner], INNER), d_taps[kernel, inner:]], 0),
            placed(d_head[1, :, 0], dt_bias.shape[0]),
            placed(d_head[0, :, 0], a_log.shape[0]),
            placed(d_skip_wide.reshape(heads, HEADDIM).sum(1), d_skip.shape[0]),
            placed((gain0 + gain1)[0], INNER),
        ]
        return jnp.concatenate([s.reshape(-1) for s in small])

    def unpack_small(packed):
        summed, at = [], 0
        for shape in shapes:
            size = 1
            for extent in shape:
                size *= extent
            summed.append(packed[at : at + size].reshape(shape))
            at += size
        return summed

    team = lay.team
    natural = (2, team, tokens)
    out_rows = INNER // (lay.parts * lay.wsh)
    in_rows = model // (lay.parts * lay.wsh)
    run = Order()

    gates, raws, turned_normed = [], [], []
    mixed, starts, edges, downs = [], [], [], []
    turned_gated, d_gates, d_raws, small_scan = [], [], [], []

    def project_step(at):
        gate, raw, flat = run(lambda v: project_tokens(v, weight, inner), normeds[at])
        gates.append(gate)
        raws.append(raw.reshape(1, length, raw.shape[-1]))
        turned_normed.append(flat)

    def forward_step(at):
        got = run(lambda p: scan_forward(raws[at], 0, p, *params[1:]), params[0])
        mixed.append(got[0].reshape(natural + (inner,)))
        starts.append(got[1])
        edges.append(got[2])

    def stats_step(at):
        down, own = run(lambda m: gate_stats(grads[at], w_out, m, gates[at], gain_own), mixed[at])
        downs.append(down)
        return own

    def back_step(at, sums):
        flat, d_mixed, d_gate, keep, send, gain = run(
            lambda v: gate_back(table, mixed[at], gates[at], downs[at], v, gain_own, w_out), sums
        )
        turned_gated.append(flat[None])
        d_gates.append(d_gate)
        return d_mixed, keep, send, gain

    def scan_step(at, d_mixed):
        d_raw, *small = run(
            lambda d: scan_backward(
                raws[at], 0, d.reshape(1, length, inner), starts[at], edges[at], *params
            ),
            d_mixed,
        )
        d_raws.append(d_raw[0])
        small_scan.append(small)

    def norm_step(at):
        return run(
            lambda v: norm_part(
                table, d_gates[at], v.reshape(natural + (v.shape[-1],)), normeds[at], weight
            ),
            d_raws[at],
        )

    def owned_parts(part):
        blocks = part.reshape(lay.parts, lay.wsh, in_rows, part.shape[1])
        kept = pick(blocks, lay.wplace, 1)
        away = [pick(blocks, (lay.wplace + d) % lay.wsh, 1) for d in range(1, lay.wsh)]
        return kept, [lay.wsh_shift(a, d + 1) for d, a in enumerate(away)]

    def to_owners(kept):
        return lax.all_to_all(kept, ALL, split_axis=0, concat_axis=0, tiled=True)

    def add_owned(kept, came):
        total = kept.astype(F32)
        for part in came:
            total = total + part.astype(F32)
        return total.astype(BF16)

    def chip_step(keep, came):
        return run(lambda v: chip_parts(core_sum(keep, v), lay), came)

    def finish(parts):
        mine, away = run(lambda v: chip_sum([v] + parts[1:], lay), parts[0])
        return mine, lay.other_half(away)

    project_step(0)
    forward_step(0)
    parts = run(lambda v: team_parts(v, lay), stats_step(0))
    sums = run(add_all, parts)
    d_mixed0, out_keep0, send, gain0 = back_step(0, sums)
    out_came0 = lay.other_core(send)
    scan_step(0, d_mixed0)
    out_parts0 = chip_step(out_keep0, out_came0)
    project_step(1)
    forward_step(1)
    own = stats_step(1)
    sum0 = finish(out_parts0)
    parts = run(lambda v: team_parts(v, lay), own)
    scan_base = run(lambda v: row_grad([(turned_normed[0], v)], F32), d_raws[0])
    keep0, send, norm_gain0 = norm_step(0)
    came0 = lay.other_core(send)
    parts, sum0 = join(parts, sum0)
    sums = run(add_all, parts)
    d_mixed1, out_keep1, send, gain1 = back_step(1, sums)
    norm_parts0 = chip_step(keep0, came0)
    out_came1 = lay.other_core(send)
    flat_gates = [d.reshape(length, inner) for d in d_gates]
    gate_grad = run(
        lambda v: row_grad([(turned_normed[0], v), (turned_normed[1], flat_gates[1])], BF16),
        flat_gates[0],
    )
    out_parts1 = chip_step(out_keep1, out_came1)
    gate_kept, gate_came = run(owned_parts, gate_grad)
    flat_grads = [g.reshape(length, model) for g in grads]
    out_grad = run(
        lambda v: row_grad([(v, flat_grads[0]), (turned_gated[1], flat_grads[1])], BF16),
        turned_gated[0],
    )
    blocks = out_grad.reshape(2, lay.wsh, out_rows, model)

    def out_split(values):
        kept = pick(values, lay.wplace, 1)
        away = [pick(values, (lay.wplace + d) % lay.wsh, 1) for d in range(1, lay.wsh)]
        return kept, [lay.wsh_shift(a, d + 1) for d, a in enumerate(away)]

    out_kept, out_came = run(out_split, blocks)
    scan_step(1, d_mixed1)
    norm_parts0, out_parts1, gate_came, out_came, run.last = join(
        norm_parts0, out_parts1, gate_came, out_came, run.last
    )
    norm0 = finish(norm_parts0)
    gate_kept = run(add_owned, gate_kept, gate_came)
    out_kept = run(add_owned, out_kept, out_came)
    cross, first_pairs, second_pairs = [], [], []
    for half in range(2):
        for chip in range(lay.chips):
            source = (half * lay.chips + chip) * 2 + half
            peer = ((1 - half) * lay.chips + chip) * 2 + half
            head_block = half * lay.chips + chip
            cross.append((peer, source))
            first_pairs.append((source, 2 * head_block))
            second_pairs.append((source, 2 * head_block + 1))
    out_came = lax.ppermute(out_kept, ALL, cross)
    sum1 = finish(out_parts1)
    keep1, send, norm_gain1 = norm_step(1)
    came1 = lay.other_core(send)
    scan_grad = run(lambda v: row_grad([(turned_normed[1], v)], BF16, None, scan_base), d_raws[1])
    scan_kept, scan_came = run(owned_parts, scan_grad)
    norm_parts1 = chip_step(keep1, came1)
    by_gate = to_owners(gate_kept)
    small = run(lambda v: pack_small(v), norm_gain1)
    small = run(lambda v: v + lay.other_core(v), small)
    small = [small] + [lay.chip_flip(small, b) for b in range(1, lay.chips)]
    scan_came, norm_parts1, by_gate, small, out_came, norm0, sum1, run.last = join(
        scan_came, norm_parts1, by_gate, small, out_came, norm0, sum1, run.last
    )
    scan_kept = run(add_owned, scan_kept, scan_came)
    by_scan = to_owners(scan_kept)
    norm1 = finish(norm_parts1)
    small = run(add_all, small)
    out_held = run(lambda v: (v.astype(F32) + out_came.astype(F32)).astype(BF16), out_kept)
    out_first = lax.ppermute(out_held[0], ALL, first_pairs)
    out_second = lax.ppermute(out_held[1], ALL, second_pairs)
    small = run(lambda v: v + lay.other_half(v), small)
    bit = 1
    while bit < lay.wsh:
        small = run(
            lambda v: v + lax.ppermute(v, "wsh", [(i, i ^ bit) for i in range(lay.wsh)]), small
        )
        bit *= 2
    out_proj_grad = run(lambda v: v.astype(F32) + out_second.astype(F32), out_first)

    def whole_place(first, second):
        mine = jnp.stack([first[0], second[0]], 0)
        other = jnp.stack([first[1], second[1]], 0)
        return both_halves(mine, other, lay)

    block_out = run(
        lambda v: (hidden_wide + whole_place((v, sum0[1]), sum1).astype(F32)).astype(BF16), sum0[0]
    )

    def hidden_step(value):
        d_scaled = whole_place((value, norm0[1]), norm1).astype(F32) * norm_gain
        inward = jnp.mean(d_scaled * hidden_wide, axis=-1, keepdims=True)
        return (
            cotangent.astype(F32)
            + norm_scale * d_scaled
            - hidden_wide * (norm_scale * norm_scale * norm_scale * inward)
        )

    hidden_grad = run(hidden_step, norm0[0])

    def assemble(scan_parts):
        def owned(parts):
            view = parts.reshape(2, team, in_rows, parts.shape[-1])
            return jnp.sum(view.astype(F32), axis=0)

        by_block = [(b % lay.chips) * 2 + b // lay.chips for b in range(team)]
        scan_sums = owned(scan_parts)
        gate_sums = owned(by_gate)
        bc_sum = jnp.sum(scan_sums[:, :, inner : inner + 2 * STATE], axis=0)
        return jnp.concatenate(
            [gate_sums[m] for m in by_block]
            + [scan_sums[m, :, :inner] for m in by_block]
            + [bc_sum]
            + [scan_sums[m, :, inner + 2 * STATE :] for m in by_block],
            1,
        )

    in_proj_grad = run(assemble, by_scan)
    ngain_all, conv_all, cbias_all, shift_all, rate_all, skip_all, ggain_all = unpack_small(small)
    return (
        block_out,
        hidden_grad,
        ngain_all,
        in_proj_grad,
        conv_all,
        cbias_all,
        shift_all,
        rate_all,
        skip_all,
        ggain_all,
        out_proj_grad,
    )


def solution(mesh):
    parts, wsh = mesh.devices.shape
    fine = Mesh(mesh.devices.reshape(2, parts // 4, 2, wsh), ("half", "chip", "core", "wsh"))
    by_token = P("wsh", ALL, None)
    by_row = P("wsh", None)
    owned = P(ALL + ("wsh",), None)
    whole = P()
    return jax.shard_map(
        shards,
        mesh=fine,
        in_specs=(by_token, by_token, whole, by_row) + (whole,) * 6 + (by_row,),
        out_specs=(by_token, by_token, whole, owned) + (whole,) * 6 + (owned,),
        check_vma=False,
    )
```

```python
import functools
import jax
import jax.numpy as jnp
from jax import lax
from jax.experimental import pallas as pl
from jax.experimental.pallas import tpu as pltpu
from jax.sharding import Mesh
from jax.sharding import PartitionSpec as P

STATE = 128
HEADDIM = 64
SPAN = 256
INNER = 4096
EPS = 1e-05
HIGH = lax.Precision.HIGHEST
NEG = -1e30
F32 = jnp.float32
BF16 = jnp.bfloat16


def dot_plain(left, right, precision=None):
    return lax.dot_general(
        left, right, (((1,), (0,)), ((), ())), preferred_element_type=F32, precision=precision
    )


def dot_lanes(left, right):
    return lax.dot_general(left, right, (((1,), (1,)), ((), ())), preferred_element_type=F32)


def dot_rows(left, right):
    return lax.dot_general(left, right, (((0,), (0,)), ((), ())), preferred_element_type=F32)


def softplus(values):
    return jnp.maximum(values, 0.0) + jnp.log1p(jnp.exp(-jnp.abs(values)))


def sigmoid(values):
    return 1.0 / (1.0 + jnp.exp(-values))


def head_rows(raw_steps, shift, neg_rate):
    span, heads = raw_steps.shape
    wide = jnp.concatenate([raw_steps, jnp.zeros((span, 128 - heads), F32)], 1)
    raw = wide.T[:heads] + shift
    step = softplus(raw)
    order = lax.broadcasted_iota(jnp.int32, (span, span), 0)
    until = lax.broadcasted_iota(jnp.int32, (span, span), 1)
    upper = jnp.where(order <= until, 1.0, 0.0)
    cum = dot_plain(step * neg_rate, upper, HIGH)
    last = cum[:, span - 1 :]
    return raw, step, cum, jnp.exp(cum), jnp.exp(last - cum)


def as_columns(rows):
    count, span = rows.shape
    return jnp.concatenate([rows, jnp.zeros((128 - count, span), F32)], 0).T


def spread_lanes(columns, start, heads):
    span = columns.shape[0]
    low = lax.broadcasted_iota(jnp.int32, (span, 2 * HEADDIM), 1) < HEADDIM
    pieces = []
    for pair in range(heads // 2):
        at = start + 2 * pair
        pieces.append(jnp.where(low, columns[:, at : at + 1], columns[:, at + 1 : at + 2]))
    return jnp.concatenate(pieces, 1)


def pair_halves(values, pair):
    slab = values[:, 2 * HEADDIM * pair : 2 * HEADDIM * (pair + 1)]
    low = lax.broadcasted_iota(jnp.int32, slab.shape, 1) < HEADDIM
    zero = jnp.zeros_like(slab)
    return slab, (jnp.where(low, slab, zero), jnp.where(low, zero, slab))


def convolve(window, taps, offset, span):
    running = None
    for k in range(taps.shape[0]):
        term = window[pl.ds(offset(k), span), :] * taps[k : k + 1, :]
        running = term if running is None else running + term
    return running


def scan_forward_body(
    heads,
    raw_ref,
    taps_ref,
    bias_ref,
    shift_ref,
    rate_ref,
    skip_ref,
    mixed_ref,
    start_ref,
    edge_ref,
    state,
    window,
):
    span = raw_ref.shape[0]
    inner = heads * HEADDIM
    wide = inner + 2 * STATE
    first = pl.program_id(1) == 0

    @pl.when(first)
    def _():
        state[...] = jnp.zeros_like(state)
        window[0:8, :] = jnp.zeros((8, wide), F32)

    @pl.when(jnp.logical_not(first))
    def _():
        window[0:8, :] = window[span : span + 8, :]

    edge_ref[...] = window[0:8, :]
    window[8 : 8 + span, :] = raw_ref[:, :wide].astype(F32)
    conv = convolve(window, taps_ref[...], lambda k: 5 + k, span) + bias_ref[...]
    act = conv * sigmoid(conv)
    x_act = act[:, :inner]
    b_low = act[:, inner : inner + STATE].astype(BF16)
    c_act = act[:, inner + STATE :]
    c_low = c_act.astype(BF16)
    c_both = jnp.concatenate([c_low, (c_act - c_low.astype(F32)).astype(BF16)], 1)
    raw, step, cum, grown, tail = head_rows(
        raw_ref[:, wide:].astype(F32), shift_ref[...], -jnp.exp(rate_ref[...])
    )
    columns = as_columns(jnp.concatenate([cum, step, grown, tail], 0))
    step_wide = spread_lanes(columns, heads, heads)
    grown_wide = spread_lanes(columns, 2 * heads, heads)
    tail_wide = spread_lanes(columns, 3 * heads, heads)
    stepped = x_act * step_wide
    stepped_low = stepped.astype(BF16)
    held = state[...]
    start_ref[...] = held
    held_low = held.astype(BF16)
    scores = dot_lanes(c_both, jnp.concatenate([b_low, b_low], 1))
    carried = dot_plain(c_both, jnp.concatenate([held_low, held_low], 0)) * grown_wide
    carried = carried + skip_ref[...] * x_act
    rows = lax.broadcasted_iota(jnp.int32, (span, span), 0)
    cols = lax.broadcasted_iota(jnp.int32, (span, span), 1)
    causal = rows >= cols
    for pair in range(heads // 2):
        _, halves = pair_halves(stepped_low, pair)
        total = carried[:, 2 * HEADDIM * pair : 2 * HEADDIM * (pair + 1)]
        for half in range(2):
            head = 2 * pair + half
            spread = columns[:, head : head + 1] - cum[head : head + 1, :]
            weights = jnp.exp(jnp.where(causal, spread, NEG)) * scores
            total = total + dot_plain(weights.astype(BF16), halves[half])
        mixed_ref[:, 2 * HEADDIM * pair : 2 * HEADDIM * (pair + 1)] = total.astype(BF16)
    fresh = dot_rows(b_low, (stepped * tail_wide).astype(BF16))
    state[...] = held * grown_wide[span - 1 : span, :] + fresh


def scan_forward(raw, at, taps, bias, shift, log_rate, skip_wide, wait=()):
    _, length, width = raw.shape
    seqs = 1
    heads = shift.shape[0]
    inner = heads * HEADDIM
    wide = inner + 2 * STATE
    spans = length // SPAN
    whole = lambda shape: pl.BlockSpec(shape, lambda s, i: (0,) * len(shape))
    return call_after(
        wait,
        functools.partial(scan_forward_body, heads),
        (raw, taps, bias, shift, log_rate, skip_wide),
        grid=(seqs, spans),
        in_specs=[
            pl.BlockSpec((None, SPAN, width), lambda s, i: (at, i, 0)),
            whole(taps.shape),
            whole(bias.shape),
            whole(shift.shape),
            whole(log_rate.shape),
            whole(skip_wide.shape),
        ],
        out_specs=[
            pl.BlockSpec((None, SPAN, inner), lambda s, i: (s, i, 0)),
            pl.BlockSpec((None, None, STATE, inner), lambda s, i: (s, i, 0, 0)),
            pl.BlockSpec((None, None, 8, wide), lambda s, i: (s, i, 0, 0)),
        ],
        out_shape=[
            jax.ShapeDtypeStruct((seqs, length, inner), BF16),
            jax.ShapeDtypeStruct((seqs, spans, STATE, inner), F32),
            jax.ShapeDtypeStruct((seqs, spans, 8, wide), F32),
        ],
        scratch_shapes=[pltpu.VMEM((STATE, inner), F32), pltpu.VMEM((SPAN + 8, wide), F32)],
        compiler_params=kernel_params(),
        cost_estimate=light_cost(10),
        name="scan_forward",
    )


def scan_backward_body(
    heads,
    raw_ref,
    down_ref,
    start_ref,
    edge_ref,
    taps_ref,
    bias_ref,
    shift_ref,
    rate_ref,
    skip_ref,
    draw_ref,
    dtaps_ref,
    dskip_ref,
    dhead_ref,
    dstate,
    window,
    ahead,
):
    span = raw_ref.shape[0]
    inner = heads * HEADDIM
    wide = inner + 2 * STATE
    step_at = pl.program_id(1)

    @pl.when((pl.program_id(0) == 0) & (step_at == 0))
    def _():
        dtaps_ref[...] = jnp.zeros_like(dtaps_ref)
        dskip_ref[...] = jnp.zeros_like(dskip_ref)
        dhead_ref[...] = jnp.zeros_like(dhead_ref)

    @pl.when(step_at == 0)
    def _():
        dstate[...] = jnp.zeros_like(dstate)
        ahead[span : span + 8, :] = jnp.zeros((8, wide), F32)

    @pl.when(step_at != 0)
    def _():
        ahead[span : span + 8, :] = ahead[0:8, :]

    taps = taps_ref[...]
    window[0:8, :] = edge_ref[...]
    window[8 : 8 + span, :] = raw_ref[:, :wide].astype(F32)
    conv = convolve(window, taps, lambda k: 5 + k, span) + bias_ref[...]
    sig = sigmoid(conv)
    act = conv * sig
    x_act = act[:, :inner]
    b_low = act[:, inner : inner + STATE].astype(BF16)
    c_low = act[:, inner + STATE :].astype(BF16)
    neg_rate = -jnp.exp(rate_ref[...])
    raw, step, cum, grown, tail = head_rows(raw_ref[:, wide:].astype(F32), shift_ref[...], neg_rate)
    columns = as_columns(jnp.concatenate([cum, step, grown, tail], 0))
    step_wide = spread_lanes(columns, heads, heads)
    grown_wide = spread_lanes(columns, 2 * heads, heads)
    tail_wide = spread_lanes(columns, 3 * heads, heads)
    stepped = x_act * step_wide
    stepped_low = stepped.astype(BF16)
    down_low = down_ref[...]
    down = down_low.astype(F32)
    held = start_ref[...]
    held_low = held.astype(BF16)
    dheld = dstate[...]
    dheld_low = dheld.astype(BF16)
    scores = dot_lanes(b_low, c_low)
    rows = lax.broadcasted_iota(jnp.int32, (span, span), 0)
    cols = lax.broadcasted_iota(jnp.int32, (span, span), 1)
    causal = cols >= rows
    dscores = jnp.zeros((span, span), F32)
    dstepped_parts = []
    gained = []
    lost = []
    for pair in range(heads // 2):
        _, x_halves = pair_halves(stepped_low, pair)
        down_pair, down_halves = pair_halves(down_low, pair)
        total = jnp.zeros((span, 2 * HEADDIM), F32)
        for half in range(2):
            head = 2 * pair + half
            spread = cum[head : head + 1, :] - columns[:, head : head + 1]
            decay = jnp.exp(jnp.where(causal, spread, NEG))
            weights = decay * scores
            dweights = dot_lanes(x_halves[half], down_pair)
            dscores = dscores + decay * dweights
            both = weights * dweights
            gained.append(jnp.sum(both, axis=0, keepdims=True))
            lost.append(jnp.sum(both, axis=1, keepdims=True))
            total = total + dot_plain(weights.astype(BF16), down_halves[half])
        dstepped_parts.append(total)
    dscores_low = dscores.astype(BF16)
    dtail = dot_plain(b_low, dheld_low) * tail_wide
    dstepped = jnp.concatenate(dstepped_parts, 1) + dtail
    down_grown = (down * grown_wide).astype(BF16)
    d_b = dot_plain(dscores_low, c_low) + dot_lanes((stepped * tail_wide).astype(BF16), dheld_low)
    d_c = dot_rows(dscores_low, b_low) + dot_lanes(down_grown, held_low)
    carried = dot_plain(c_low, held_low) * grown_wide
    member = lax.broadcasted_iota(jnp.int32, (heads, inner), 1) // HEADDIM
    which = lax.broadcasted_iota(jnp.int32, (heads, inner), 0)
    pick = jnp.where(member == which, 1.0, 0.0)
    pick_low = pick.astype(BF16)
    carried_sum = dot_lanes(pick_low, (down * carried).astype(BF16))
    tail_sum = dot_lanes(pick_low, (stepped * dtail).astype(BF16))
    step_sum = dot_lanes(pick_low, (x_act * dstepped).astype(BF16))
    lost_rows = as_columns_back(jnp.concatenate(lost, 1))
    state_sum = jnp.sum(pick * jnp.sum(held * dheld, axis=0, keepdims=True), axis=1, keepdims=True)
    dcum = jnp.concatenate(gained, 0) + carried_sum - lost_rows - tail_sum
    since = jnp.where(rows >= cols, 1.0, 0.0)
    whole_part = jnp.sum(tail_sum, axis=1, keepdims=True) + grown[:, span - 1 :] * state_sum
    dlog = dot_plain(dcum, since, HIGH) + whole_part
    draw_step = (step_sum + neg_rate * dlog) * sigmoid(raw)
    dhead_ref[0] += neg_rate * jnp.sum(step * dlog, axis=1, keepdims=True)
    dhead_ref[1] += jnp.sum(draw_step, axis=1, keepdims=True)
    dskip_ref[...] += jnp.sum(down * x_act, axis=0, keepdims=True)
    d_x = dstepped * step_wide + skip_ref[...] * down
    dconv = jnp.concatenate([d_x, d_b, d_c], 1) * (sig * (1.0 + conv * (1.0 - sig)))
    ahead[0:span, :] = dconv
    draw = convolve(ahead, taps, lambda k: 3 - k, span)
    draw_ref[:, :wide] = draw.astype(BF16)
    draw_ref[:, wide:] = as_columns(draw_step)[:, :heads].astype(BF16)
    for k in range(taps.shape[0]):
        dtaps_ref[k : k + 1, :] += jnp.sum(
            dconv * window[pl.ds(5 + k, span), :], axis=0, keepdims=True
        )
    dtaps_ref[4:5, :] += jnp.sum(dconv, axis=0, keepdims=True)
    dstate[...] = dheld * grown_wide[span - 1 : span, :] + dot_rows(c_low, down_grown)


def as_columns_back(columns):
    span, heads = columns.shape
    return jnp.concatenate([columns, jnp.zeros((span, 128 - heads), F32)], 1).T[:heads]


def scan_backward(raw, at, down, starts, edges, taps, bias, shift, log_rate, skip_wide, wait=()):
    _, length, width = raw.shape
    seqs = 1
    heads = shift.shape[0]
    inner = heads * HEADDIM
    wide = inner + 2 * STATE
    spans = length // SPAN
    whole = lambda shape: pl.BlockSpec(shape, lambda s, i: (0,) * len(shape))
    turned = lambda s, i: (s, spans - 1 - i, 0)
    return call_after(
        wait,
        functools.partial(scan_backward_body, heads),
        (raw, down, starts, edges, taps, bias, shift, log_rate, skip_wide),
        grid=(seqs, spans),
        in_specs=[
            pl.BlockSpec((None, SPAN, width), lambda s, i: (at, spans - 1 - i, 0)),
            pl.BlockSpec((None, SPAN, inner), turned),
            pl.BlockSpec((None, None, STATE, inner), lambda s, i: (s, spans - 1 - i, 0, 0)),
            pl.BlockSpec((None, None, 8, wide), lambda s, i: (s, spans - 1 - i, 0, 0)),
            whole(taps.shape),
            whole(bias.shape),
            whole(shift.shape),
            whole(log_rate.shape),
            whole(skip_wide.shape),
        ],
        out_specs=[
            pl.BlockSpec((None, SPAN, width), turned),
            whole((8, wide)),
            whole((1, inner)),
            whole((2, heads, 1)),
        ],
        out_shape=[
            jax.ShapeDtypeStruct((seqs, length, width), BF16),
            jax.ShapeDtypeStruct((8, wide), F32),
            jax.ShapeDtypeStruct((1, inner), F32),
            jax.ShapeDtypeStruct((2, heads, 1), F32),
        ],
        scratch_shapes=[
            pltpu.VMEM((STATE, inner), F32),
            pltpu.VMEM((SPAN + 8, wide), F32),
            pltpu.VMEM((SPAN + 8, wide), F32),
        ],
        compiler_params=kernel_params(),
        cost_estimate=light_cost(22),
        name="scan_backward",
    )

def kernel_params():
    return pltpu.CompilerParams(vmem_limit_bytes=58 * 1024 * 1024)


def call_after(wait, body, values, in_specs, **rest):
    held = [pl.BlockSpec(memory_space=pl.ANY)] * len(wait)

    def inner_body(*refs):
        body(*refs[: len(values)], *refs[len(values) + len(wait) :])

    return pl.pallas_call(inner_body, in_specs=list(in_specs) + held, **rest)(*values, *wait)


def light_cost(micros):
    work = int(micros * 1e9 * 1.0)
    return pl.CostEstimate(flops=work, bytes_accessed=work // 400, transcendentals=0)


def project_body(inner, tokens_ref, weight_ref, gate_ref, raw_ref, turned_ref):
    _, _, tokens, model = tokens_ref.shape
    values = tokens_ref[...].reshape(4 * tokens, model)
    put_by_member(gate_ref, dot_lanes(values, weight_ref[:inner, :]))
    put_by_member(raw_ref, dot_lanes(values, weight_ref[inner:, :]))
    for half in range(2):
        pair = jnp.concatenate([tokens_ref[core, half] for core in range(2)], 0)
        turned_ref[half] = pair.T


def project_tokens(values, weight, inner, wait=()):
    team, _, tokens, model = values.shape
    width = weight.shape[0]

    def natural(size):
        return pl.BlockSpec((2, 2, tokens, size), lambda i: (0, i, 0, 0))

    return call_after(
        wait,
        functools.partial(project_body, inner),
        (values, weight),
        grid=(team // 2,),
        in_specs=[
            pl.BlockSpec((2, 2, tokens, model), lambda i: (i, 0, 0, 0)),
            pl.BlockSpec((width, model), lambda i: (0, 0)),
        ],
        out_specs=[
            natural(inner),
            natural(width - inner),
            pl.BlockSpec((2, model, 2 * tokens), lambda i: (0, 0, i)),
        ],
        out_shape=[
            jax.ShapeDtypeStruct((2, team, tokens, inner), BF16),
            jax.ShapeDtypeStruct((2, team, tokens, width - inner), BF16),
            jax.ShapeDtypeStruct((2, model, team * tokens), BF16),
        ],
        compiler_params=kernel_params(),
        cost_estimate=light_cost(11),
        name="project_tokens",
    )


def by_member(ref):
    return jnp.concatenate(
        [ref[half, member] for member in range(ref.shape[1]) for half in range(2)], 0
    )


def put_by_member(ref, rows):
    tokens = ref.shape[2]
    for member in range(ref.shape[1]):
        for half in range(2):
            at = (member * 2 + half) * tokens
            ref[half, member] = rows[at : at + tokens].astype(ref.dtype)


def gate_stats_body(grad_ref, weight_ref, mixed_ref, gate_ref, gain_ref, down_ref, sums_ref):
    pair, _, tokens, model = grad_ref.shape
    d_gated = dot_lanes(grad_ref[...].reshape(pair * 2 * tokens, model), weight_ref[...])
    gate = by_member(gate_ref).astype(F32)
    unit = by_member(mixed_ref).astype(F32) * gate * sigmoid(gate)
    put_by_member(down_ref, d_gated)
    square = jnp.sum(unit * unit, axis=1, keepdims=True)
    cross = jnp.sum(d_gated * gain_ref[...] * unit, axis=1, keepdims=True)
    sums_ref[...] = as_columns_back(jnp.concatenate([square, cross], 1))


def gate_stats(grad, weight, mixed, gate, gain, wait=()):
    team, _, tokens, model = grad.shape
    inner = weight.shape[0]
    pair = 2
    rows = pair * 2 * tokens
    natural = pl.BlockSpec((2, pair, tokens, inner), lambda i: (0, i, 0, 0))
    return call_after(
        wait,
        gate_stats_body,
        (grad, weight, mixed, gate, gain),
        grid=(team // pair,),
        in_specs=[
            pl.BlockSpec((pair, 2, tokens, model), lambda i: (i, 0, 0, 0)),
            pl.BlockSpec((inner, model), lambda i: (0, 0)),
            natural,
            natural,
            pl.BlockSpec((1, inner), lambda i: (0, 0)),
        ],
        out_specs=[
            natural,
            pl.BlockSpec((2, rows), lambda i: (0, i)),
        ],
        out_shape=[
            jax.ShapeDtypeStruct((2, team, tokens, inner), F32),
            jax.ShapeDtypeStruct((2, team * 2 * tokens), F32),
        ],
        compiler_params=kernel_params(),
        cost_estimate=light_cost(7),
        name="gate_stats",
    )


def gate_back_body(
    mixed_ref,
    gate_ref,
    down_ref,
    sums_ref,
    gain_ref,
    weight_ref,
    turned_ref,
    d_mixed_ref,
    d_gate_ref,
    out_ref,
    d_gain_ref,
):
    @pl.when(pl.program_id(0) == 0)
    def _():
        d_gain_ref[...] = jnp.zeros_like(d_gain_ref)

    columns = as_columns(sums_ref[...])
    gain = gain_ref[...]
    scale = lax.rsqrt(columns[:, 0:1] / INNER + EPS)
    pull = columns[:, 1:2] * (scale * scale * scale / INNER)
    mixed = by_member(mixed_ref).astype(F32)
    gate = by_member(gate_ref).astype(F32)
    down = by_member(down_ref)
    sig = sigmoid(gate)
    act = gate * sig
    unit = mixed * act
    scaled = unit * scale
    gated_wide = scaled * gain
    turned_ref[...] = gated_wide.T.astype(BF16)
    out_ref[...] = dot_plain(gated_wide.astype(BF16), weight_ref[...]).astype(BF16)
    d_unit = down * gain * scale - unit * pull
    put_by_member(d_mixed_ref, d_unit * act)
    put_by_member(d_gate_ref, d_unit * mixed * (sig * (1.0 + gate * (1.0 - sig))))
    d_gain_ref[...] += jnp.sum(down * scaled, axis=0, keepdims=True)


def gate_back(mixed, gate, down, sums, gain, weight, wait=()):
    _, team, tokens, inner = down.shape
    model = weight.shape[1]
    rows = 4 * tokens
    natural = pl.BlockSpec((2, 2, tokens, inner), lambda i: (0, i, 0, 0))
    one = pl.BlockSpec((1, inner), lambda i: (0, 0))
    return call_after(
        wait,
        gate_back_body,
        (mixed, gate, down, sums, gain, weight),
        grid=(team // 2,),
        in_specs=[
            natural,
            natural,
            natural,
            pl.BlockSpec((2, rows), lambda i: (0, i)),
            one,
            pl.BlockSpec((inner, model), lambda i: (0, 0)),
        ],
        out_specs=[
            pl.BlockSpec((inner, rows), lambda i: (0, i)),
            natural,
            natural,
            pl.BlockSpec((rows, model), lambda i: (i, 0)),
            one,
        ],
        out_shape=[
            jax.ShapeDtypeStruct((inner, team * 2 * tokens), BF16),
            jax.ShapeDtypeStruct((2, team, tokens, inner), BF16),
            jax.ShapeDtypeStruct((2, team, tokens, inner), BF16),
            jax.ShapeDtypeStruct((team * 2 * tokens, model), BF16),
            jax.ShapeDtypeStruct((1, inner), F32),
        ],
        compiler_params=kernel_params(),
        cost_estimate=light_cost(8),
        name="gate_back",
    )


def row_grad_body(pairs, cols, has_base, *refs):
    out_ref = refs[-1]
    total = None
    for k in range(pairs):
        left_ref = refs[2 * k]
        right_ref = refs[2 * k + 1]
        count, _, depth = left_ref.shape
        for part in range(count):
            right = right_ref[part * depth : (part + 1) * depth, :]
            if cols is not None:
                right = right[:, cols[0] : cols[1]]
            term = dot_plain(left_ref[part], right)
            total = term if total is None else total + term
    if has_base:
        base = refs[2 * pairs][...]
        if cols is not None:
            base = base[:, cols[0] : cols[1]]
        total = total + base
    out_ref[...] = total.astype(out_ref.dtype)


def row_grad(operands, kind, cols=None, base=None, wait=()):
    rows = operands[0][0].shape[1]
    width = operands[0][1].shape[1]
    got = width if cols is None else cols[1] - cols[0]
    tile = min(512, rows)
    if got > 1024:
        tile = min(256, rows)
    specs, args = [], []
    for left, right in operands:
        specs.append(pl.BlockSpec((left.shape[0], tile, left.shape[2]), lambda i: (0, i, 0)))
        specs.append(pl.BlockSpec(right.shape, lambda i: (0, 0)))
        args += [left, right]
    if base is not None:
        specs.append(pl.BlockSpec((tile, width), lambda i: (i, 0)))
        args.append(base)
    return call_after(
        wait,
        functools.partial(row_grad_body, len(operands), cols, base is not None),
        tuple(args),
        grid=(rows // tile,),
        in_specs=specs,
        out_specs=pl.BlockSpec((tile, got), lambda i: (i, 0)),
        out_shape=jax.ShapeDtypeStruct((rows, got), kind),
        compiler_params=kernel_params(),
        cost_estimate=light_cost(8),
        name="row_grad",
    )


def norm_part_body(d_gate_ref, d_raw_ref, normed_ref, weight_ref, out_ref, gain_ref):
    @pl.when(pl.program_id(0) == 0)
    def _():
        gain_ref[...] = jnp.zeros_like(gain_ref)

    inner = d_gate_ref.shape[-1]
    part = dot_plain(by_member(d_gate_ref), weight_ref[:inner, :])
    part = part + dot_plain(by_member(d_raw_ref), weight_ref[inner:, :])
    normed = normed_ref[...].reshape(out_ref.shape).astype(F32)
    gain_ref[...] += jnp.sum(part * normed, axis=0, keepdims=True)
    out_ref[...] = part.astype(BF16)


def norm_part(d_gate, d_raw, normed, weight, wait=()):
    _, team, tokens, inner = d_gate.shape
    width = d_raw.shape[-1]
    model = weight.shape[1]
    rows = 4 * tokens

    def natural(size):
        return pl.BlockSpec((2, 2, tokens, size), lambda i: (0, i, 0, 0))

    return call_after(
        wait,
        norm_part_body,
        (d_gate, d_raw, normed, weight),
        grid=(team // 2,),
        in_specs=[
            natural(inner),
            natural(width),
            pl.BlockSpec((2, 2, tokens, model), lambda i: (i, 0, 0, 0)),
            pl.BlockSpec((inner + width, model), lambda i: (0, 0)),
        ],
        out_specs=[
            pl.BlockSpec((rows, model), lambda i: (i, 0)),
            pl.BlockSpec((1, model), lambda i: (0, 0)),
        ],
        out_shape=[
            jax.ShapeDtypeStruct((team * 2 * tokens, model), BF16),
            jax.ShapeDtypeStruct((1, model), F32),
        ],
        compiler_params=kernel_params(),
        cost_estimate=light_cost(11),
        name="norm_part",
    )


TEAM = ("chip", "core")
ALL = ("half", "chip", "core")
EVERY = ALL + ("wsh",)


def join(*values):
    leaves, tree = jax.tree.flatten(values)
    anywhere = [pl.BlockSpec(memory_space=pl.ANY)] * len(leaves)
    out = pl.pallas_call(
        lambda *refs: None,
        in_specs=anywhere,
        out_specs=anywhere,
        out_shape=[jax.ShapeDtypeStruct(v.shape, v.dtype) for v in leaves],
        input_output_aliases={k: k for k in range(len(leaves))},
        cost_estimate=light_cost(0),
        name="join",
    )(*leaves)
    return jax.tree.unflatten(tree, out)


class Layout:
    def __init__(self):
        self.chips = lax.axis_size("chip")
        self.wsh = lax.axis_size("wsh")
        self.team = 2 * self.chips
        self.parts = 2 * self.team
        self.half = lax.axis_index("half")
        self.chip = lax.axis_index("chip")
        self.core = lax.axis_index("core")
        self.wplace = lax.axis_index("wsh")
        self.member = self.chip * 2 + self.core
        self.block = self.core * self.chips + self.chip

    def other_core(self, values):
        return lax.ppermute(values, "core", [(0, 1), (1, 0)])

    def other_half(self, values):
        return lax.ppermute(values, "half", [(0, 1), (1, 0)])

    def chip_flip(self, values, bits):
        return lax.ppermute(values, "chip", [(i, i ^ bits) for i in range(self.chips)])

    def wsh_shift(self, values, shift):
        size = self.wsh
        return lax.ppermute(values, "wsh", [(i, (i + shift) % size) for i in range(size)])


def pick(values, at, axis):
    return lax.dynamic_index_in_dim(values, at, axis, keepdims=False)


def split_halves(own, lay):
    count = own.shape[0] // 2
    keep = lax.dynamic_slice_in_dim(own, lay.half * count, count, 0)
    away = lax.dynamic_slice_in_dim(own, (1 - lay.half) * count, count, 0)
    return keep, away


def team_gather(keep, came, lay):
    pair = jnp.where(lay.half == 0, jnp.stack([keep, came]), jnp.stack([came, keep]))
    return lax.all_gather(pair, TEAM, axis=0)


def both_halves(mine, other, lay):
    first = jnp.where(lay.half == 0, mine, other)
    second = jnp.where(lay.half == 0, other, mine)
    return jnp.concatenate([first, second], 0)


def team_sum(part, lay):
    own = lax.psum_scatter(part, TEAM, scatter_dimension=0, tiled=True)
    return own.reshape(2, own.shape[0] // 2, own.shape[1])


def two_halves(own, lay):
    return pick(own, lay.half, 0), lay.other_half(pick(own, 1 - lay.half, 0))


def columns_in_place(local, came, lay):
    wide = local.shape[1]
    full = jnp.zeros((local.shape[0], lay.wsh * wide), local.dtype)
    full = lax.dynamic_update_slice_in_dim(full, local, lay.wplace * wide, 1)
    for start, pieces in came:
        for shift, piece in enumerate(pieces):
            at = ((lay.wplace - shift - 1) % lay.wsh) * wide
            full = lax.dynamic_update_slice(full, piece, (start, at))
    return full


def team_parts(values, lay):
    values = values + lay.other_core(values)
    return [values] + [lay.chip_flip(values, bits) for bits in range(1, lay.chips)]


def add_all(parts):
    while len(parts) > 1:
        parts = [parts[k] + parts[k + 1] for k in range(0, len(parts), 2)]
    return parts[0]


def shards(
    hidden,
    cotangent,
    norm_gain,
    in_proj,
    conv_weight,
    conv_bias,
    dt_bias,
    a_log,
    d_skip,
    gate_gain,
    out_proj,
):
    lay = Layout()
    seqs, tokens, model = hidden.shape
    count = seqs // 2
    length = tokens * lay.parts
    inner = INNER // lay.team
    heads = inner // HEADDIM
    block = lay.block
    steps_at = 2 * INNER + 2 * STATE

    def columns(values, start, width, axis=1):
        return lax.dynamic_slice_in_dim(values, start, width, axis)

    hidden_wide = hidden.astype(F32)
    norm_scale = lax.rsqrt(jnp.mean(hidden_wide * hidden_wide, axis=-1, keepdims=True) + EPS)
    normed = (hidden_wide * norm_scale * norm_gain).astype(BF16)

    turned = in_proj.T
    local = jnp.concatenate(
        [
            columns(turned, block * inner, inner, 0),
            columns(turned, INNER + block * inner, inner, 0),
            turned[2 * INNER : steps_at],
            columns(turned, steps_at + block * heads, heads, 0),
        ],
        0,
    )

    def to_wsh(values):
        return [lay.wsh_shift(values, shift) for shift in range(1, lay.wsh)]

    cut = (inner // 128 + 1) * 128
    keep, away = split_halves(normed, lay)
    keep_grad, away_grad = split_halves(cotangent, lay)
    came_first, came, later, away_grad = join(
        to_wsh(local[:cut]), lay.other_half(away), local[cut:], away_grad
    )
    normeds = [team_gather(keep[0], came[0], lay)]
    rows_held = INNER // lay.wsh
    owner = (block * inner) // rows_held
    at_row = jnp.where(owner == lay.wplace, block * inner - owner * rows_held, 0)
    rows_here = columns(out_proj, at_row, inner, 0)
    came_last, came_grad, rows_here = join(to_wsh(later), lay.other_half(away_grad), rows_here)
    weight = columns_in_place(local, [(0, came_first), (cut, came_last)], lay)
    out_pieces = []
    for shift in range(1, lay.wsh):
        pairs = []
        for place in range(lay.team):
            head_block = (place % 2) * lay.chips + place // 2
            holder = (head_block * inner) // rows_held
            source = place * lay.wsh + holder
            pairs.append((source, place * lay.wsh + (holder + shift) % lay.wsh))
        out_pieces.append(lax.ppermute(rows_here, TEAM + ("wsh",), pairs))

    def own_rows(first, *rest):
        total = jnp.where(owner == lay.wplace, rows_here, jnp.zeros_like(rows_here)) + first
        for piece in rest:
            total = total + piece
        return total

    grads = [team_gather(keep_grad[0], came_grad[0], lay)]
    for s in range(1, count):
        normeds.append(team_gather(keep[s], came[s], lay))
        grads.append(team_gather(keep_grad[s], came_grad[s], lay))

    taps = jnp.concatenate(
        [columns(conv_weight, block * inner, inner), conv_weight[:, INNER:]], 1
    )
    bias = jnp.concatenate([columns(conv_bias, block * inner, inner, 0), conv_bias[INNER:]], 0)
    shift_own = columns(dt_bias, block * heads, heads, 0)[:, None]
    rate_own = columns(a_log, block * heads, heads, 0)[:, None]
    skip_own = jnp.repeat(columns(d_skip, block * heads, heads, 0), HEADDIM)[None]
    gain_own = columns(gate_gain, block * inner, inner, 0)[None]
    params = (taps, bias[None], shift_own, rate_own, skip_own)

    kernel = conv_weight.shape[0]
    shapes = [norm_gain.shape, conv_weight.shape, conv_bias.shape]
    shapes += [dt_bias.shape, a_log.shape, d_skip.shape, gate_gain.shape]

    def placed(values, width):
        full = jnp.zeros(values.shape[:-1] + (width,), F32)
        return lax.dynamic_update_slice_in_dim(
            full, values, block * values.shape[-1], values.ndim - 1
        )

    def pack_small(norm_gain1):
        d_taps, d_skip_wide, d_head = jax.tree.map(lambda *v: sum(v[1:], v[0]), *small_scan)
        small = [
            (norm_gain0 + norm_gain1)[0] / norm_gain,
            jnp.concatenate([placed(d_taps[:kernel, :inner], INNER), d_taps[:kernel, inner:]], 1),
            jnp.concatenate([placed(d_taps[kernel, :inner], INNER), d_taps[kernel, inner:]], 0),
            placed(d_head[1, :, 0], dt_bias.shape[0]),
            placed(d_head[0, :, 0], a_log.shape[0]),
            placed(d_skip_wide.reshape(heads, HEADDIM).sum(1), d_skip.shape[0]),
            placed((gain0 + gain1)[0], INNER),
        ]
        return jnp.concatenate([s.reshape(-1) for s in small])

    def unpack_small(packed):
        summed, at = [], 0
        for shape in shapes:
            size = 1
            for extent in shape:
                size *= extent
            summed.append(packed[at : at + size].reshape(shape))
            at += size
        return summed

    team = lay.team
    natural = (2, team, tokens)
    out_rows = INNER // (lay.parts * lay.wsh)
    in_rows = model // (lay.parts * lay.wsh)

    gates, raws, turned_normed = [], [], []
    mixed, starts, edges, downs = [], [], [], []
    turned_gated, d_gates, d_raws, small_scan = [], [], [], []

    def project_step(at, wait=()):
        gate, raw, flat = project_tokens(normeds[at], weight, inner, wait)
        gates.append(gate)
        raws.append(raw.reshape(1, length, raw.shape[-1]))
        turned_normed.append(flat)

    def forward_step(at, wait=()):
        got = scan_forward(raws[at], 0, *params, wait=wait)
        mixed.append(got[0].reshape(natural + (inner,)))
        starts.append(got[1])
        edges.append(got[2])

    def stats_step(at, wait=()):
        down, own = gate_stats(grads[at], w_out, mixed[at], gates[at], gain_own, wait)
        downs.append(down)
        return own

    def back_step(at, sums, wait=()):
        flat, d_mixed, d_gate, out, gain = gate_back(
            mixed[at], gates[at], downs[at], sums, gain_own, w_out, wait
        )
        turned_gated.append(flat[None])
        d_gates.append(d_gate)
        return d_mixed, out, gain

    def scan_step(at, d_mixed, wait=()):
        d_mixed = d_mixed.reshape(1, length, inner)
        d_raw, *small = scan_backward(
            raws[at], 0, d_mixed, starts[at], edges[at], *params, wait=wait
        )
        d_raws.append(d_raw[0])
        small_scan.append(small)

    def norm_step(at, wait=()):
        d_raw = d_raws[at].reshape(natural + (d_raws[at].shape[-1],))
        return norm_part(d_gates[at], d_raw, normeds[at], weight, wait)

    def owned_parts(part):
        blocks = part.reshape(lay.parts, lay.wsh, in_rows, part.shape[1])
        kept = pick(blocks, lay.wplace, 1)
        away = [pick(blocks, (lay.wplace + d) % lay.wsh, 1) for d in range(1, lay.wsh)]
        return kept, [lay.wsh_shift(a, d + 1) for d, a in enumerate(away)]

    def to_owners(kept):
        return lax.all_to_all(kept, ALL, split_axis=0, concat_axis=0, tiled=True)

    def add_owned(kept, came):
        total = kept.astype(F32)
        for part in came:
            total = total + part.astype(F32)
        return total.astype(BF16)

    flat_grads = [g.reshape(length, model) for g in grads]
    cross, first_pairs, second_pairs = [], [], []
    for half in range(2):
        for chip in range(lay.chips):
            source = (half * lay.chips + chip) * 2 + half
            peer = ((1 - half) * lay.chips + chip) * 2 + half
            head_block = half * lay.chips + chip
            cross.append((peer, source))
            first_pairs.append((source, 2 * head_block))
            second_pairs.append((source, 2 * head_block + 1))

    def out_split(values):
        values = values.reshape(2, lay.wsh, out_rows, model)
        kept = pick(values, lay.wplace, 1)
        away = [pick(values, (lay.wplace + d) % lay.wsh, 1) for d in range(1, lay.wsh)]
        return kept, [lay.wsh_shift(a, d + 1) for d, a in enumerate(away)]

    def over_groups(values):
        parts = []
        for bits in range(lay.wsh):
            moved = values
            if bits:
                pairs = [(i, i ^ bits) for i in range(lay.wsh)]
                moved = lax.ppermute(values, "wsh", pairs)
            both = [(h * lay.wsh + i, (1 - h) * lay.wsh + (i ^ bits)) for h in range(2) for i in range(lay.wsh)]
            parts += [moved, lax.ppermute(values, ("half", "wsh"), both)]
        return parts

    project_step(0)
    forward_step(0)
    out_pieces, mixed[0] = join(out_pieces, mixed[0])
    w_out = own_rows(*out_pieces)
    sums = add_all(team_parts(stats_step(0), lay))
    d_mixed0, out, gain0 = back_step(0, sums)
    out0 = team_sum(out, lay)
    scan_step(0, d_mixed0)
    project_step(1, (small_scan[0][1],))
    forward_step(1)
    own = stats_step(1)
    parts = team_parts(own, lay)
    part, norm_gain0 = norm_step(0, (own,))
    norm0 = team_sum(part, lay)
    sums = add_all(parts)
    d_mixed1, out, gain1 = back_step(1, sums, (norm_gain0,))
    out1 = team_sum(out, lay)
    flat_gates = [d.reshape(length, inner) for d in d_gates]
    gate_grad = row_grad(
        [(turned_normed[0], flat_gates[0]), (turned_normed[1], flat_gates[1])], BF16
    )
    gate_kept, gate_came = owned_parts(gate_grad)
    out_grad = row_grad(
        [(turned_gated[0], flat_grads[0]), (turned_gated[1], flat_grads[1])],
        BF16,
        wait=(gate_kept,),
    )
    out_kept, out_came = out_split(out_grad)
    scan_base = row_grad([(turned_normed[0], d_raws[0])], F32, wait=(out_kept,))
    gate_came, sum0, d_mixed1, scan_base = join(
        gate_came, two_halves(out0, lay), d_mixed1, scan_base
    )
    by_gate = to_owners(add_owned(gate_kept, gate_came))
    scan_step(1, d_mixed1)
    part, norm_gain1 = norm_step(1)
    norm1 = team_sum(part, lay)
    out_came, sum1, norm_gain1 = join(out_came, two_halves(out1, lay), norm_gain1)
    scan_grad = row_grad(
        [(turned_normed[1], d_raws[1])], BF16, None, scan_base, wait=(norm_gain1,)
    )
    scan_kept, scan_came = owned_parts(scan_grad)
    out_kept = add_owned(out_kept, out_came)
    out_came = lax.ppermute(out_kept, ALL, cross)
    small = add_all(team_parts(pack_small(norm_gain1), lay))
    scan_came, norm0, small = join(scan_came, two_halves(norm0, lay), small)
    by_scan = to_owners(add_owned(scan_kept, scan_came))
    out_held = (out_kept.astype(F32) + out_came.astype(F32)).astype(BF16)
    out_first = lax.ppermute(out_held[0], ALL, first_pairs)
    out_second = lax.ppermute(out_held[1], ALL, second_pairs)
    norm1 = two_halves(norm1, lay)
    small = add_all(over_groups(small))
    out_proj_grad = out_first.astype(F32) + out_second.astype(F32)

    def whole_place(first, second):
        mine = jnp.stack([first[0], second[0]], 0)
        other = jnp.stack([first[1], second[1]], 0)
        return both_halves(mine, other, lay)

    block_out = (hidden_wide + whole_place(sum0, sum1).astype(F32)).astype(BF16)

    def hidden_step():
        d_scaled = whole_place(norm0, norm1).astype(F32) * norm_gain
        inward = jnp.mean(d_scaled * hidden_wide, axis=-1, keepdims=True)
        return (
            cotangent.astype(F32)
            + norm_scale * d_scaled
            - hidden_wide * (norm_scale * norm_scale * norm_scale * inward)
        )

    hidden_grad = hidden_step()

    def assemble(scan_parts):
        def owned(parts):
            view = parts.reshape(2, team, in_rows, parts.shape[-1])
            return jnp.sum(view.astype(F32), axis=0)

        by_block = [(b % lay.chips) * 2 + b // lay.chips for b in range(team)]
        scan_sums = owned(scan_parts)
        gate_sums = owned(by_gate)
        bc_sum = jnp.sum(scan_sums[:, :, inner : inner + 2 * STATE], axis=0)
        return jnp.concatenate(
            [gate_sums[m] for m in by_block]
            + [scan_sums[m, :, :inner] for m in by_block]
            + [bc_sum]
            + [scan_sums[m, :, inner + 2 * STATE :] for m in by_block],
            1,
        )

    in_proj_grad = assemble(by_scan)
    ngain_all, conv_all, cbias_all, shift_all, rate_all, skip_all, ggain_all = unpack_small(small)
    return (
        block_out,
        hidden_grad,
        ngain_all,
        in_proj_grad,
        conv_all,
        cbias_all,
        shift_all,
        rate_all,
        skip_all,
        ggain_all,
        out_proj_grad,
    )


def solution(mesh):
    parts, wsh = mesh.devices.shape
    fine = Mesh(mesh.devices.reshape(2, parts // 4, 2, wsh), ("half", "chip", "core", "wsh"))
    by_token = P("wsh", ALL, None)
    by_row = P("wsh", None)
    owned = P(ALL + ("wsh",), None)
    whole = P()
    return jax.shard_map(
        shards,
        mesh=fine,
        in_specs=(by_token, by_token, whole, by_row) + (whole,) * 6 + (by_row,),
        out_specs=(by_token, by_token, whole, owned) + (whole,) * 6 + (owned,),
        check_vma=False,
    )
```

```python
import functools
import jax
import jax.numpy as jnp
from jax import lax
from jax.experimental import pallas as pl
from jax.experimental.pallas import tpu as pltpu
from jax.sharding import Mesh
from jax.sharding import PartitionSpec as P

STATE = 128
HEADDIM = 64
SPAN = 256
INNER = 4096
EPS = 1e-05
HIGH = lax.Precision.HIGHEST
NEG = -1e30
F32 = jnp.float32
BF16 = jnp.bfloat16


def dot_plain(left, right, precision=None):
    return lax.dot_general(
        left, right, (((1,), (0,)), ((), ())), preferred_element_type=F32, precision=precision
    )


def dot_lanes(left, right):
    return lax.dot_general(left, right, (((1,), (1,)), ((), ())), preferred_element_type=F32)


def dot_rows(left, right):
    return lax.dot_general(left, right, (((0,), (0,)), ((), ())), preferred_element_type=F32)


def softplus(values):
    return jnp.maximum(values, 0.0) + jnp.log1p(jnp.exp(-jnp.abs(values)))


def sigmoid(values):
    return 1.0 / (1.0 + jnp.exp(-values))


def head_rows(raw_steps, shift, neg_rate):
    span, heads = raw_steps.shape
    wide = jnp.concatenate([raw_steps, jnp.zeros((span, 128 - heads), F32)], 1)
    raw = wide.T[:heads] + shift
    step = softplus(raw)
    order = lax.broadcasted_iota(jnp.int32, (span, span), 0)
    until = lax.broadcasted_iota(jnp.int32, (span, span), 1)
    upper = jnp.where(order <= until, 1.0, 0.0)
    cum = dot_plain(step * neg_rate, upper, HIGH)
    last = cum[:, span - 1 :]
    return raw, step, cum, jnp.exp(cum), jnp.exp(last - cum)


def as_columns(rows):
    count, span = rows.shape
    return jnp.concatenate([rows, jnp.zeros((128 - count, span), F32)], 0).T


def spread_lanes(columns, start, heads):
    span = columns.shape[0]
    low = lax.broadcasted_iota(jnp.int32, (span, 2 * HEADDIM), 1) < HEADDIM
    pieces = []
    for pair in range(heads // 2):
        at = start + 2 * pair
        pieces.append(jnp.where(low, columns[:, at : at + 1], columns[:, at + 1 : at + 2]))
    return jnp.concatenate(pieces, 1)


def pair_halves(values, pair):
    slab = values[:, 2 * HEADDIM * pair : 2 * HEADDIM * (pair + 1)]
    low = lax.broadcasted_iota(jnp.int32, slab.shape, 1) < HEADDIM
    zero = jnp.zeros_like(slab)
    return slab, (jnp.where(low, slab, zero), jnp.where(low, zero, slab))


def convolve(window, taps, offset, span):
    running = None
    for k in range(taps.shape[0]):
        term = window[pl.ds(offset(k), span), :] * taps[k : k + 1, :]
        running = term if running is None else running + term
    return running


def scan_forward_body(
    heads,
    half_ref,
    raw_ref,
    taps_ref,
    bias_ref,
    shift_ref,
    rate_ref,
    skip_ref,
    mixed_ref,
    start_ref,
    edge_ref,
    state,
    window,
):
    span = raw_ref.shape[0]
    inner = heads * HEADDIM
    wide = inner + 2 * STATE
    first = pl.program_id(1) == 0

    @pl.when(first)
    def _():
        state[...] = jnp.zeros_like(state)
        window[0:8, :] = jnp.zeros((8, wide), F32)

    @pl.when(jnp.logical_not(first))
    def _():
        window[0:8, :] = window[span : span + 8, :]

    edge_ref[...] = window[0:8, :]
    window[8 : 8 + span, :] = raw_ref[:, :wide].astype(F32)
    conv = convolve(window, taps_ref[...], lambda k: 5 + k, span) + bias_ref[...]
    act = conv * sigmoid(conv)
    x_act = act[:, :inner]
    b_low = act[:, inner : inner + STATE].astype(BF16)
    c_act = act[:, inner + STATE :]
    c_low = c_act.astype(BF16)
    c_both = jnp.concatenate([c_low, (c_act - c_low.astype(F32)).astype(BF16)], 1)
    raw, step, cum, grown, tail = head_rows(
        raw_ref[:, wide:].astype(F32), shift_ref[...], -jnp.exp(rate_ref[...])
    )
    columns = as_columns(jnp.concatenate([cum, step, grown, tail], 0))
    step_wide = spread_lanes(columns, heads, heads)
    grown_wide = spread_lanes(columns, 2 * heads, heads)
    tail_wide = spread_lanes(columns, 3 * heads, heads)
    stepped = x_act * step_wide
    stepped_low = stepped.astype(BF16)
    held = state[...]
    start_ref[...] = held
    held_low = held.astype(BF16)
    scores = dot_lanes(c_both, jnp.concatenate([b_low, b_low], 1))
    carried = dot_plain(c_both, jnp.concatenate([held_low, held_low], 0)) * grown_wide
    carried = carried + skip_ref[...] * x_act
    rows = lax.broadcasted_iota(jnp.int32, (span, span), 0)
    cols = lax.broadcasted_iota(jnp.int32, (span, span), 1)
    causal = rows >= cols
    for pair in range(heads // 2):
        _, halves = pair_halves(stepped_low, pair)
        total = carried[:, 2 * HEADDIM * pair : 2 * HEADDIM * (pair + 1)]
        for half in range(2):
            head = 2 * pair + half
            spread = columns[:, head : head + 1] - cum[head : head + 1, :]
            weights = jnp.exp(jnp.where(causal, spread, NEG)) * scores
            total = total + dot_plain(weights.astype(BF16), halves[half])
        mixed_ref[:, 2 * HEADDIM * pair : 2 * HEADDIM * (pair + 1)] = total.astype(BF16)
    fresh = dot_rows(b_low, (stepped * tail_wide).astype(BF16))
    state[...] = held * grown_wide[span - 1 : span, :] + fresh


def scan_forward(half, raw, at, taps, bias, shift, log_rate, skip_wide, wait=()):
    _, length, width = raw.shape
    seqs = 1
    heads = shift.shape[0]
    inner = heads * HEADDIM
    wide = inner + 2 * STATE
    spans = length // SPAN
    whole = lambda shape: pl.BlockSpec(shape, lambda s, i, t: (0,) * len(shape))
    lies = lambda i, t: (i + t[0] * (spans // 2)) % spans
    return call_after(
        wait,
        functools.partial(scan_forward_body, heads),
        (half, raw, taps, bias, shift, log_rate, skip_wide),
        scalars=1,
        grid=(seqs, spans),
        in_specs=[
            pl.BlockSpec((None, SPAN, width), lambda s, i, t: (at, lies(i, t), 0)),
            whole(taps.shape),
            whole(bias.shape),
            whole(shift.shape),
            whole(log_rate.shape),
            whole(skip_wide.shape),
        ],
        out_specs=[
            pl.BlockSpec((None, SPAN, inner), lambda s, i, t: (s, lies(i, t), 0)),
            pl.BlockSpec((None, None, STATE, inner), lambda s, i, t: (s, i, 0, 0)),
            pl.BlockSpec((None, None, 8, wide), lambda s, i, t: (s, i, 0, 0)),
        ],
        out_shape=[
            jax.ShapeDtypeStruct((seqs, length, inner), BF16),
            jax.ShapeDtypeStruct((seqs, spans, STATE, inner), F32),
            jax.ShapeDtypeStruct((seqs, spans, 8, wide), F32),
        ],
        scratch_shapes=[pltpu.VMEM((STATE, inner), F32), pltpu.VMEM((SPAN + 8, wide), F32)],
        compiler_params=kernel_params(),
        cost_estimate=light_cost(10),
        name="scan_forward",
    )


def scan_backward_body(
    heads,
    half_ref,
    raw_ref,
    down_ref,
    start_ref,
    edge_ref,
    taps_ref,
    bias_ref,
    shift_ref,
    rate_ref,
    skip_ref,
    draw_ref,
    dtaps_ref,
    dskip_ref,
    dhead_ref,
    dstate,
    window,
    ahead,
):
    span = raw_ref.shape[0]
    inner = heads * HEADDIM
    wide = inner + 2 * STATE
    step_at = pl.program_id(1)

    @pl.when((pl.program_id(0) == 0) & (step_at == 0))
    def _():
        dtaps_ref[...] = jnp.zeros_like(dtaps_ref)
        dskip_ref[...] = jnp.zeros_like(dskip_ref)
        dhead_ref[...] = jnp.zeros_like(dhead_ref)

    @pl.when(step_at == 0)
    def _():
        dstate[...] = jnp.zeros_like(dstate)
        ahead[span : span + 8, :] = jnp.zeros((8, wide), F32)

    @pl.when(step_at != 0)
    def _():
        ahead[span : span + 8, :] = ahead[0:8, :]

    taps = taps_ref[...]
    window[0:8, :] = edge_ref[...]
    window[8 : 8 + span, :] = raw_ref[:, :wide].astype(F32)
    conv = convolve(window, taps, lambda k: 5 + k, span) + bias_ref[...]
    sig = sigmoid(conv)
    act = conv * sig
    x_act = act[:, :inner]
    b_low = act[:, inner : inner + STATE].astype(BF16)
    c_low = act[:, inner + STATE :].astype(BF16)
    neg_rate = -jnp.exp(rate_ref[...])
    raw, step, cum, grown, tail = head_rows(raw_ref[:, wide:].astype(F32), shift_ref[...], neg_rate)
    columns = as_columns(jnp.concatenate([cum, step, grown, tail], 0))
    step_wide = spread_lanes(columns, heads, heads)
    grown_wide = spread_lanes(columns, 2 * heads, heads)
    tail_wide = spread_lanes(columns, 3 * heads, heads)
    stepped = x_act * step_wide
    stepped_low = stepped.astype(BF16)
    down_low = down_ref[...]
    down = down_low.astype(F32)
    held = start_ref[...]
    held_low = held.astype(BF16)
    dheld = dstate[...]
    dheld_low = dheld.astype(BF16)
    scores = dot_lanes(b_low, c_low)
    rows = lax.broadcasted_iota(jnp.int32, (span, span), 0)
    cols = lax.broadcasted_iota(jnp.int32, (span, span), 1)
    causal = cols >= rows
    dscores = jnp.zeros((span, span), F32)
    dstepped_parts = []
    gained = []
    lost = []
    for pair in range(heads // 2):
        _, x_halves = pair_halves(stepped_low, pair)
        down_pair, down_halves = pair_halves(down_low, pair)
        total = jnp.zeros((span, 2 * HEADDIM), F32)
        for half in range(2):
            head = 2 * pair + half
            spread = cum[head : head + 1, :] - columns[:, head : head + 1]
            decay = jnp.exp(jnp.where(causal, spread, NEG))
            weights = decay * scores
            dweights = dot_lanes(x_halves[half], down_pair)
            dscores = dscores + decay * dweights
            both = weights * dweights
            gained.append(jnp.sum(both, axis=0, keepdims=True))
            lost.append(jnp.sum(both, axis=1, keepdims=True))
            total = total + dot_plain(weights.astype(BF16), down_halves[half])
        dstepped_parts.append(total)
    dscores_low = dscores.astype(BF16)
    dtail = dot_plain(b_low, dheld_low) * tail_wide
    dstepped = jnp.concatenate(dstepped_parts, 1) + dtail
    down_grown = (down * grown_wide).astype(BF16)
    d_b = dot_plain(dscores_low, c_low) + dot_lanes((stepped * tail_wide).astype(BF16), dheld_low)
    d_c = dot_rows(dscores_low, b_low) + dot_lanes(down_grown, held_low)
    carried = dot_plain(c_low, held_low) * grown_wide
    member = lax.broadcasted_iota(jnp.int32, (heads, inner), 1) // HEADDIM
    which = lax.broadcasted_iota(jnp.int32, (heads, inner), 0)
    pick = jnp.where(member == which, 1.0, 0.0)
    pick_low = pick.astype(BF16)
    carried_sum = dot_lanes(pick_low, (down * carried).astype(BF16))
    tail_sum = dot_lanes(pick_low, (stepped * dtail).astype(BF16))
    step_sum = dot_lanes(pick_low, (x_act * dstepped).astype(BF16))
    lost_rows = as_columns_back(jnp.concatenate(lost, 1))
    state_sum = jnp.sum(pick * jnp.sum(held * dheld, axis=0, keepdims=True), axis=1, keepdims=True)
    dcum = jnp.concatenate(gained, 0) + carried_sum - lost_rows - tail_sum
    since = jnp.where(rows >= cols, 1.0, 0.0)
    whole_part = jnp.sum(tail_sum, axis=1, keepdims=True) + grown[:, span - 1 :] * state_sum
    dlog = dot_plain(dcum, since, HIGH) + whole_part
    draw_step = (step_sum + neg_rate * dlog) * sigmoid(raw)
    dhead_ref[0] += neg_rate * jnp.sum(step * dlog, axis=1, keepdims=True)
    dhead_ref[1] += jnp.sum(draw_step, axis=1, keepdims=True)
    dskip_ref[...] += jnp.sum(down * x_act, axis=0, keepdims=True)
    d_x = dstepped * step_wide + skip_ref[...] * down
    dconv = jnp.concatenate([d_x, d_b, d_c], 1) * (sig * (1.0 + conv * (1.0 - sig)))
    ahead[0:span, :] = dconv
    draw = convolve(ahead, taps, lambda k: 3 - k, span)
    draw_ref[:, :wide] = draw.astype(BF16)
    draw_ref[:, wide:] = as_columns(draw_step)[:, :heads].astype(BF16)
    for k in range(taps.shape[0]):
        dtaps_ref[k : k + 1, :] += jnp.sum(
            dconv * window[pl.ds(5 + k, span), :], axis=0, keepdims=True
        )
    dtaps_ref[4:5, :] += jnp.sum(dconv, axis=0, keepdims=True)
    dstate[...] = dheld * grown_wide[span - 1 : span, :] + dot_rows(c_low, down_grown)


def as_columns_back(columns):
    span, heads = columns.shape
    return jnp.concatenate([columns, jnp.zeros((span, 128 - heads), F32)], 1).T[:heads]


def scan_backward(half, raw, at, down, starts, edges, taps, bias, shift, log_rate, skip_wide, wait=()):
    _, length, width = raw.shape
    seqs = 1
    heads = shift.shape[0]
    inner = heads * HEADDIM
    wide = inner + 2 * STATE
    spans = length // SPAN
    whole = lambda shape: pl.BlockSpec(shape, lambda s, i, t: (0,) * len(shape))
    lies = lambda i, t: (spans - 1 - i + t[0] * (spans // 2)) % spans
    turned = lambda s, i, t: (s, lies(i, t), 0)
    return call_after(
        wait,
        functools.partial(scan_backward_body, heads),
        (half, raw, down, starts, edges, taps, bias, shift, log_rate, skip_wide),
        scalars=1,
        grid=(seqs, spans),
        in_specs=[
            pl.BlockSpec((None, SPAN, width), lambda s, i, t: (at, lies(i, t), 0)),
            pl.BlockSpec((None, SPAN, inner), turned),
            pl.BlockSpec((None, None, STATE, inner), lambda s, i, t: (s, spans - 1 - i, 0, 0)),
            pl.BlockSpec((None, None, 8, wide), lambda s, i, t: (s, spans - 1 - i, 0, 0)),
            whole(taps.shape),
            whole(bias.shape),
            whole(shift.shape),
            whole(log_rate.shape),
            whole(skip_wide.shape),
        ],
        out_specs=[
            pl.BlockSpec((None, SPAN, width), turned),
            whole((8, wide)),
            whole((1, inner)),
            whole((2, heads, 1)),
        ],
        out_shape=[
            jax.ShapeDtypeStruct((seqs, length, width), BF16),
            jax.ShapeDtypeStruct((8, wide), F32),
            jax.ShapeDtypeStruct((1, inner), F32),
            jax.ShapeDtypeStruct((2, heads, 1), F32),
        ],
        scratch_shapes=[
            pltpu.VMEM((STATE, inner), F32),
            pltpu.VMEM((SPAN + 8, wide), F32),
            pltpu.VMEM((SPAN + 8, wide), F32),
        ],
        compiler_params=kernel_params(),
        cost_estimate=light_cost(22),
        name="scan_backward",
    )

def kernel_params():
    return pltpu.CompilerParams(vmem_limit_bytes=58 * 1024 * 1024)


def call_after(wait, body, values, in_specs, scalars=0, **rest):
    held = [pl.BlockSpec(memory_space=pl.ANY)] * len(wait)

    def inner_body(*refs):
        body(*refs[: len(values)], *refs[len(values) + len(wait) :])

    if scalars:
        rest["grid_spec"] = pltpu.PrefetchScalarGridSpec(
            num_scalar_prefetch=scalars,
            grid=rest.pop("grid"),
            in_specs=list(in_specs) + held,
            out_specs=rest.pop("out_specs"),
            scratch_shapes=rest.pop("scratch_shapes"),
        )
    else:
        rest["in_specs"] = list(in_specs) + held
    return pl.pallas_call(inner_body, **rest)(*values, *wait)


def light_cost(micros):
    work = int(micros * 1e9 * 1.0)
    return pl.CostEstimate(flops=work, bytes_accessed=work // 400, transcendentals=0)


def both_parts(near_ref, far_ref):
    return jnp.concatenate(
        [ref[member] for member in range(near_ref.shape[0]) for ref in (near_ref, far_ref)], 0
    )


def gathered(values, at):
    _, _, tokens, width = values.shape
    return pl.BlockSpec((2, None, tokens, width), lambda i: (i, at, 0, 0))


def project_body(inner, near_ref, far_ref, weight_ref, gate_ref, raw_ref, turned_ref):
    values = both_parts(near_ref, far_ref)
    put_by_member(gate_ref, dot_lanes(values, weight_ref[:inner, :]))
    put_by_member(raw_ref, dot_lanes(values, weight_ref[inner:, :]))
    for half, ref in enumerate((near_ref, far_ref)):
        turned_ref[half] = jnp.concatenate([ref[0], ref[1]], 0).T


def project_tokens(near, far, at, weight, inner, wait=()):
    team, _, tokens, model = near.shape
    width = weight.shape[0]

    def halves(size):
        return pl.BlockSpec((2, 2, tokens, size), lambda i: (0, i, 0, 0))

    return call_after(
        wait,
        functools.partial(project_body, inner),
        (near, far, weight),
        grid=(team // 2,),
        in_specs=[
            gathered(near, at),
            gathered(far, at),
            pl.BlockSpec((width, model), lambda i: (0, 0)),
        ],
        out_specs=[
            halves(inner),
            halves(width - inner),
            pl.BlockSpec((2, model, 2 * tokens), lambda i: (0, 0, i)),
        ],
        out_shape=[
            jax.ShapeDtypeStruct((2, team, tokens, inner), BF16),
            jax.ShapeDtypeStruct((2, team, tokens, width - inner), BF16),
            jax.ShapeDtypeStruct((2, model, team * tokens), BF16),
        ],
        compiler_params=kernel_params(),
        cost_estimate=light_cost(11),
        name="project_tokens",
    )


def by_member(ref):
    return jnp.concatenate(
        [ref[half, member] for member in range(ref.shape[1]) for half in range(2)], 0
    )


def put_by_member(ref, rows):
    tokens = ref.shape[2]
    for member in range(ref.shape[1]):
        for half in range(2):
            at = (member * 2 + half) * tokens
            ref[half, member] = rows[at : at + tokens].astype(ref.dtype)


def gate_stats_body(near_ref, far_ref, weight_ref, mixed_ref, gate_ref, gain_ref, down_ref, sums_ref):
    d_gated = dot_lanes(both_parts(near_ref, far_ref), weight_ref[...])
    gate = by_member(gate_ref).astype(F32)
    unit = by_member(mixed_ref).astype(F32) * gate * sigmoid(gate)
    put_by_member(down_ref, d_gated)
    square = jnp.sum(unit * unit, axis=1, keepdims=True)
    cross = jnp.sum(d_gated * gain_ref[...] * unit, axis=1, keepdims=True)
    sums_ref[...] = as_columns_back(jnp.concatenate([square, cross], 1))


def gate_stats(near, near_at, far, far_at, weight, mixed, gate, gain, wait=()):
    team, _, tokens, model = near.shape
    inner = weight.shape[0]
    pair = 2
    rows = pair * 2 * tokens
    natural = pl.BlockSpec((2, pair, tokens, inner), lambda i: (0, i, 0, 0))
    return call_after(
        wait,
        gate_stats_body,
        (near, far, weight, mixed, gate, gain),
        grid=(team // pair,),
        in_specs=[
            gathered(near, near_at),
            gathered(far, far_at),
            pl.BlockSpec((inner, model), lambda i: (0, 0)),
            natural,
            natural,
            pl.BlockSpec((1, inner), lambda i: (0, 0)),
        ],
        out_specs=[
            natural,
            pl.BlockSpec((2, rows), lambda i: (0, i)),
        ],
        out_shape=[
            jax.ShapeDtypeStruct((2, team, tokens, inner), F32),
            jax.ShapeDtypeStruct((2, team * 2 * tokens), F32),
        ],
        compiler_params=kernel_params(),
        cost_estimate=light_cost(7),
        name="gate_stats",
    )


def gate_back_body(
    mixed_ref,
    gate_ref,
    down_ref,
    sums_ref,
    gain_ref,
    weight_ref,
    turned_ref,
    d_mixed_ref,
    d_gate_ref,
    out_ref,
    d_gain_ref,
):
    @pl.when(pl.program_id(0) == 0)
    def _():
        d_gain_ref[...] = jnp.zeros_like(d_gain_ref)

    columns = as_columns(sums_ref[...])
    gain = gain_ref[...]
    scale = lax.rsqrt(columns[:, 0:1] / INNER + EPS)
    pull = columns[:, 1:2] * (scale * scale * scale / INNER)
    mixed = by_member(mixed_ref).astype(F32)
    gate = by_member(gate_ref).astype(F32)
    down = by_member(down_ref)
    sig = sigmoid(gate)
    act = gate * sig
    unit = mixed * act
    scaled = unit * scale
    gated_wide = scaled * gain
    tokens = mixed_ref.shape[2]
    for half in range(2):
        rows = [gated_wide[(2 * m + half) * tokens : (2 * m + half + 1) * tokens] for m in range(2)]
        turned_ref[half] = jnp.concatenate(rows, 0).T.astype(BF16)
    out_ref[...] = dot_plain(gated_wide.astype(BF16), weight_ref[...]).astype(BF16)
    d_unit = down * gain * scale - unit * pull
    put_by_member(d_mixed_ref, d_unit * act)
    put_by_member(d_gate_ref, d_unit * mixed * (sig * (1.0 + gate * (1.0 - sig))))
    d_gain_ref[...] += jnp.sum(down * scaled, axis=0, keepdims=True)


def gate_back(mixed, gate, down, sums, gain, weight, wait=()):
    _, team, tokens, inner = down.shape
    model = weight.shape[1]
    rows = 4 * tokens
    natural = pl.BlockSpec((2, 2, tokens, inner), lambda i: (0, i, 0, 0))
    one = pl.BlockSpec((1, inner), lambda i: (0, 0))
    return call_after(
        wait,
        gate_back_body,
        (mixed, gate, down, sums, gain, weight),
        grid=(team // 2,),
        in_specs=[
            natural,
            natural,
            natural,
            pl.BlockSpec((2, rows), lambda i: (0, i)),
            one,
            pl.BlockSpec((inner, model), lambda i: (0, 0)),
        ],
        out_specs=[
            pl.BlockSpec((2, inner, 2 * tokens), lambda i: (0, 0, i)),
            natural,
            natural,
            pl.BlockSpec((rows, model), lambda i: (i, 0)),
            one,
        ],
        out_shape=[
            jax.ShapeDtypeStruct((2, inner, team * tokens), BF16),
            jax.ShapeDtypeStruct((2, team, tokens, inner), BF16),
            jax.ShapeDtypeStruct((2, team, tokens, inner), BF16),
            jax.ShapeDtypeStruct((team * 2 * tokens, model), BF16),
            jax.ShapeDtypeStruct((1, inner), F32),
        ],
        compiler_params=kernel_params(),
        cost_estimate=light_cost(8),
        name="gate_back",
    )


def row_grad_body(pairs, cols, has_base, *refs):
    out_ref = refs[-1]
    total = None
    for k in range(pairs):
        left_ref = refs[2 * k]
        right_ref = refs[2 * k + 1]
        count, _, depth = left_ref.shape
        for part in range(count):
            right = right_ref[part * depth : (part + 1) * depth, :]
            if cols is not None:
                right = right[:, cols[0] : cols[1]]
            term = dot_plain(left_ref[part], right)
            total = term if total is None else total + term
    if has_base:
        base = refs[2 * pairs][...]
        if cols is not None:
            base = base[:, cols[0] : cols[1]]
        total = total + base
    out_ref[...] = total.astype(out_ref.dtype)


def row_grad(operands, kind, cols=None, base=None, wait=()):
    rows = operands[0][0].shape[1]
    width = operands[0][1].shape[1]
    got = width if cols is None else cols[1] - cols[0]
    tile = min(512, rows)
    if got > 1024:
        tile = min(256, rows)
    specs, args = [], []
    for left, right in operands:
        specs.append(pl.BlockSpec((left.shape[0], tile, left.shape[2]), lambda i: (0, i, 0)))
        specs.append(pl.BlockSpec(right.shape, lambda i: (0, 0)))
        args += [left, right]
    if base is not None:
        specs.append(pl.BlockSpec((tile, width), lambda i: (i, 0)))
        args.append(base)
    return call_after(
        wait,
        functools.partial(row_grad_body, len(operands), cols, base is not None),
        tuple(args),
        grid=(rows // tile,),
        in_specs=specs,
        out_specs=pl.BlockSpec((tile, got), lambda i: (i, 0)),
        out_shape=jax.ShapeDtypeStruct((rows, got), kind),
        compiler_params=kernel_params(),
        cost_estimate=light_cost(0),
        name="row_grad",
    )


def norm_part_body(d_gate_ref, d_raw_ref, near_ref, far_ref, weight_ref, out_ref, gain_ref):
    @pl.when(pl.program_id(0) == 0)
    def _():
        gain_ref[...] = jnp.zeros_like(gain_ref)

    inner = d_gate_ref.shape[-1]
    part = dot_plain(by_member(d_gate_ref), weight_ref[:inner, :])
    part = part + dot_plain(by_member(d_raw_ref), weight_ref[inner:, :])
    normed = both_parts(near_ref, far_ref).astype(F32)
    gain_ref[...] += jnp.sum(part * normed, axis=0, keepdims=True)
    out_ref[...] = part.astype(BF16)


def norm_part(d_gate, d_raw, near, far, at, weight, wait=()):
    _, team, tokens, inner = d_gate.shape
    width = d_raw.shape[-1]
    model = weight.shape[1]
    rows = 4 * tokens

    def natural(size):
        return pl.BlockSpec((2, 2, tokens, size), lambda i: (0, i, 0, 0))

    return call_after(
        wait,
        norm_part_body,
        (d_gate, d_raw, near, far, weight),
        grid=(team // 2,),
        in_specs=[
            natural(inner),
            natural(width),
            gathered(near, at),
            gathered(far, at),
            pl.BlockSpec((inner + width, model), lambda i: (0, 0)),
        ],
        out_specs=[
            pl.BlockSpec((rows, model), lambda i: (i, 0)),
            pl.BlockSpec((1, model), lambda i: (0, 0)),
        ],
        out_shape=[
            jax.ShapeDtypeStruct((team * 2 * tokens, model), BF16),
            jax.ShapeDtypeStruct((1, model), F32),
        ],
        compiler_params=kernel_params(),
        cost_estimate=light_cost(0),
        name="norm_part",
    )


def out_grad_body(seqs, *refs):
    lefts = refs[:seqs]
    near_ref, far_ref, out_ref = refs[seqs:]
    depth = lefts[0].shape[2]
    tile = out_ref.shape[1]
    total = None
    for s in range(seqs):
        for half, ref in enumerate((near_ref, far_ref)):
            term = dot_plain(lefts[s][half], ref[:, s].reshape(depth, tile))
            total = term if total is None else total + term
    out_ref[...] = total.astype(out_ref.dtype)


def out_grad_part(lefts, near, far, wait=()):
    team, seqs, tokens, model = near.shape
    inner = lefts[0].shape[1]
    tile = 256
    part = pl.BlockSpec((team, seqs, tokens, tile), lambda i: (0, 0, 0, i))
    return call_after(
        wait,
        functools.partial(out_grad_body, seqs),
        (*lefts, near, far),
        grid=(model // tile,),
        in_specs=[pl.BlockSpec(left.shape, lambda i: (0, 0, 0)) for left in lefts] + [part, part],
        out_specs=pl.BlockSpec((inner, tile), lambda i: (0, i)),
        out_shape=jax.ShapeDtypeStruct((inner, model), BF16),
        compiler_params=kernel_params(),
        cost_estimate=light_cost(8),
        name="out_grad_part",
    )


def owned_rows_body(order, inner, gate_ref, scan_ref, out_ref):
    team = len(order)
    width = scan_ref.shape[-1]
    steps = width - inner - 2 * STATE
    shared = None
    for place, member in enumerate(order):
        gate = gate_ref[0, member].astype(F32) + gate_ref[1, member].astype(F32)
        scan = scan_ref[0, member].astype(F32) + scan_ref[1, member].astype(F32)
        out_ref[:, place * inner : (place + 1) * inner] = gate
        out_ref[:, (team + place) * inner : (team + place + 1) * inner] = scan[:, :inner]
        term = scan[:, inner : inner + 2 * STATE]
        shared = term if shared is None else shared + term
        at = 2 * team * inner + 2 * STATE + place * steps
        out_ref[:, at : at + steps] = scan[:, inner + 2 * STATE :]
    out_ref[:, 2 * team * inner : 2 * team * inner + 2 * STATE] = shared


def owned_rows(order, gate, scan):
    _, team, rows, inner = gate.shape
    steps = scan.shape[-1] - inner - 2 * STATE
    total = team * (2 * inner + steps) + 2 * STATE
    return pl.pallas_call(
        functools.partial(owned_rows_body, order, inner),
        out_shape=jax.ShapeDtypeStruct((rows, total), F32),
        compiler_params=kernel_params(),
        cost_estimate=light_cost(3),
        name="owned_rows",
    )(gate, scan)


TEAM = ("chip", "core")
ALL = ("half", "chip", "core")
EVERY = ALL + ("wsh",)


def join(*values):
    leaves, tree = jax.tree.flatten(values)
    anywhere = [pl.BlockSpec(memory_space=pl.ANY)] * len(leaves)
    out = pl.pallas_call(
        lambda *refs: None,
        in_specs=anywhere,
        out_specs=anywhere,
        out_shape=[jax.ShapeDtypeStruct(v.shape, v.dtype) for v in leaves],
        input_output_aliases={k: k for k in range(len(leaves))},
        cost_estimate=light_cost(0),
        name="join",
    )(*leaves)
    return jax.tree.unflatten(tree, out)


class Layout:
    def __init__(self):
        self.chips = lax.axis_size("chip")
        self.wsh = lax.axis_size("wsh")
        self.team = 2 * self.chips
        self.parts = 2 * self.team
        self.half = lax.axis_index("half")
        self.chip = lax.axis_index("chip")
        self.core = lax.axis_index("core")
        self.wplace = lax.axis_index("wsh")
        self.member = self.chip * 2 + self.core
        self.block = self.core * self.chips + self.chip

    def other_core(self, values):
        return lax.ppermute(values, "core", [(0, 1), (1, 0)])

    def other_half(self, values):
        return lax.ppermute(values, "half", [(0, 1), (1, 0)])

    def chip_flip(self, values, bits):
        return lax.ppermute(values, "chip", [(i, i ^ bits) for i in range(self.chips)])

    def wsh_shift(self, values, shift):
        size = self.wsh
        return lax.ppermute(values, "wsh", [(i, (i + shift) % size) for i in range(size)])


def pick(values, at, axis):
    return lax.dynamic_index_in_dim(values, at, axis, keepdims=False)


def split_halves(own, lay):
    count = own.shape[0] // 2
    keep = lax.dynamic_slice_in_dim(own, lay.half * count, count, 0)
    away = lax.dynamic_slice_in_dim(own, (1 - lay.half) * count, count, 0)
    return keep, away


def team_gather(values):
    return lax.all_gather(values, TEAM, axis=0)


def both_halves(mine, other, lay):
    first = jnp.where(lay.half == 0, mine, other)
    second = jnp.where(lay.half == 0, other, mine)
    return jnp.concatenate([first, second], 0)


def team_sum(part):
    own = lax.psum_scatter(part, TEAM, scatter_dimension=0, tiled=True)
    return own.reshape(2, own.shape[0] // 2, own.shape[1])


def two_halves(own, lay):
    return own[0], lay.other_half(own[1])


def columns_in_place(local, came, lay):
    blocks = []
    for place in range(lay.wsh):
        block = local
        for shift, piece in enumerate(came):
            block = jnp.where((lay.wplace - shift - 1) % lay.wsh == place, piece, block)
        blocks.append(block)
    return jnp.concatenate(blocks, 1)


def team_parts(values, lay):
    values = values + lay.other_core(values)
    return [values] + [lay.chip_flip(values, bits) for bits in range(1, lay.chips)]


def add_all(parts):
    while len(parts) > 1:
        parts = [parts[k] + parts[k + 1] for k in range(0, len(parts), 2)]
    return parts[0]


def shards(
    hidden,
    cotangent,
    norm_gain,
    in_proj,
    conv_weight,
    conv_bias,
    dt_bias,
    a_log,
    d_skip,
    gate_gain,
    out_proj,
):
    lay = Layout()
    seqs, tokens, model = hidden.shape
    count = seqs // 2
    length = tokens * lay.parts
    inner = INNER // lay.team
    heads = inner // HEADDIM
    block = lay.block
    steps_at = 2 * INNER + 2 * STATE

    def columns(values, start, width, axis=1):
        return lax.dynamic_slice_in_dim(values, start, width, axis)

    hidden_wide = hidden.astype(F32)
    norm_scale = lax.rsqrt(jnp.mean(hidden_wide * hidden_wide, axis=-1, keepdims=True) + EPS)
    normed = (hidden_wide * norm_scale * norm_gain).astype(BF16)

    turned = in_proj.T
    local = jnp.concatenate(
        [
            columns(turned, block * inner, inner, 0),
            columns(turned, INNER + block * inner, inner, 0),
            turned[2 * INNER : steps_at],
            columns(turned, steps_at + block * heads, heads, 0),
        ],
        0,
    )

    def to_wsh(values):
        return [lay.wsh_shift(values, shift) for shift in range(1, lay.wsh)]

    cut = (inner // 128 + 1) * 128
    keep, away = split_halves(normed, lay)
    keep_grad, away_grad = split_halves(cotangent, lay)
    came_first, came, later, away_grad = join(
        to_wsh(local[:cut]), lay.other_half(away), local[cut:], away_grad
    )
    normed_near = team_gather(keep)
    normed_far = team_gather(came)
    rows_held = INNER // lay.wsh
    owner = (block * inner) // rows_held
    at_row = jnp.where(owner == lay.wplace, block * inner - owner * rows_held, 0)
    rows_here = columns(out_proj, at_row, inner, 0)
    came_last, came_grad, rows_here, normed_near = join(
        to_wsh(later), lay.other_half(away_grad), rows_here, normed_near
    )
    pieces = [jnp.concatenate(parts, 0) for parts in zip(came_first, came_last)]
    weight = columns_in_place(local, pieces, lay)
    out_pieces = []
    for shift in range(1, lay.wsh):
        pairs = []
        for place in range(lay.team):
            head_block = (place % 2) * lay.chips + place // 2
            holder = (head_block * inner) // rows_held
            source = place * lay.wsh + holder
            pairs.append((source, place * lay.wsh + (holder + shift) % lay.wsh))
        out_pieces.append(lax.ppermute(rows_here, TEAM + ("wsh",), pairs))

    def own_rows(first, *rest):
        total = jnp.where(owner == lay.wplace, rows_here, jnp.zeros_like(rows_here)) + first
        for piece in rest:
            total = total + piece
        return total

    taps = jnp.concatenate(
        [columns(conv_weight, block * inner, inner), conv_weight[:, INNER:]], 1
    )
    bias = jnp.concatenate([columns(conv_bias, block * inner, inner, 0), conv_bias[INNER:]], 0)
    shift_own = columns(dt_bias, block * heads, heads, 0)[:, None]
    rate_own = columns(a_log, block * heads, heads, 0)[:, None]
    skip_own = jnp.repeat(columns(d_skip, block * heads, heads, 0), HEADDIM)[None]
    gain_own = columns(gate_gain, block * inner, inner, 0)[None]
    params = (taps, bias[None], shift_own, rate_own, skip_own)
    normed_far, keep_grad, came_grad, weight, params, gain_own = join(
        normed_far, keep_grad, came_grad, weight, params, gain_own
    )
    grad_near = team_gather(keep_grad)
    grad_far = team_gather(came_grad)

    kernel = conv_weight.shape[0]
    shapes = [norm_gain.shape, conv_weight.shape, conv_bias.shape]
    shapes += [dt_bias.shape, a_log.shape, d_skip.shape, gate_gain.shape]

    def placed(values, width):
        full = jnp.zeros(values.shape[:-1] + (width,), F32)
        return lax.dynamic_update_slice_in_dim(
            full, values, block * values.shape[-1], values.ndim - 1
        )

    def own_small(norm_gain1):
        d_taps, d_skip_wide, d_head = jax.tree.map(lambda *v: sum(v[1:], v[0]), *small_scan)
        parts = [
            (norm_gain0 + norm_gain1)[0] / norm_gain,
            d_taps[: kernel + 1],
            d_head[:, :, 0],
            d_skip_wide.reshape(heads, HEADDIM).sum(1),
            (gain0 + gain1)[0],
        ]
        return jnp.concatenate([p.reshape(-1) for p in parts])

    def pack_small(own):
        sizes = [model, (kernel + 1) * (inner + 2 * STATE), 2 * heads, heads, inner]
        pieces, at = [], 0
        for size in sizes:
            pieces.append(own[at : at + size])
            at += size
        gain, d_taps, d_head, d_skip, d_gain = pieces
        d_taps = d_taps.reshape(kernel + 1, inner + 2 * STATE)
        d_taps = jnp.concatenate([placed(d_taps[:, :inner], INNER), d_taps[:, inner:]], 1)
        d_head = placed(d_head.reshape(2, heads), dt_bias.shape[0])
        small = [
            gain,
            d_taps[:kernel],
            d_taps[kernel],
            d_head[1],
            d_head[0],
            placed(d_skip, dt_bias.shape[0]),
            placed(d_gain, INNER),
        ]
        return jnp.concatenate([s.reshape(-1) for s in small])

    def unpack_small(packed):
        summed, at = [], 0
        for shape in shapes:
            size = 1
            for extent in shape:
                size *= extent
            summed.append(packed[at : at + size].reshape(shape))
            at += size
        return summed

    team = lay.team
    natural = (2, team, tokens)
    half_at = lay.half[None].astype(jnp.int32)
    out_rows = INNER // (lay.parts * lay.wsh)
    in_rows = model // (lay.parts * lay.wsh)

    gates, raws, turned_normed = [], [], []
    mixed, starts, edges, downs = [], [], [], []
    turned_gated, d_gates, d_raws, small_scan = [], [], [], []

    def project_step(at, wait=()):
        gate, raw, flat = project_tokens(normed_near, normed_far, at, weight, inner, wait)
        gates.append(gate)
        raws.append(raw.reshape(1, length, raw.shape[-1]))
        turned_normed.append(flat)

    def forward_step(at, wait=()):
        got = scan_forward(half_at, raws[at], 0, *params, wait=wait)
        mixed.append(got[0].reshape(natural + (inner,)))
        starts.append(got[1])
        edges.append(got[2])

    def stats_step(at, wait=()):
        down, own = gate_stats(
            grad_near, at, grad_far, at, w_out, mixed[at], gates[at], gain_own, wait
        )
        downs.append(down)
        return own

    def back_step(at, sums, wait=()):
        flat, d_mixed, d_gate, out, gain = gate_back(
            mixed[at], gates[at], downs[at], sums, gain_own, w_out, wait
        )
        turned_gated.append(flat)
        d_gates.append(d_gate)
        return d_mixed, out, gain

    def scan_step(at, d_mixed, wait=()):
        d_mixed = d_mixed.reshape(1, length, inner)
        d_raw, *small = scan_backward(
            half_at, raws[at], 0, d_mixed, starts[at], edges[at], *params, wait=wait
        )
        d_raws.append(d_raw[0])
        small_scan.append(small)

    def norm_step(at, wait=()):
        d_raw = d_raws[at].reshape(natural + (d_raws[at].shape[-1],))
        return norm_part(d_gates[at], d_raw, normed_near, normed_far, at, weight, wait)

    def owned_parts(part):
        blocks = part.reshape(lay.parts, lay.wsh, in_rows, part.shape[1])
        kept = pick(blocks, lay.wplace, 1)
        away = [pick(blocks, (lay.wplace + d) % lay.wsh, 1) for d in range(1, lay.wsh)]
        return kept, [lay.wsh_shift(a, d + 1) for d, a in enumerate(away)]

    def to_owners(kept):
        return lax.all_to_all(kept, ALL, split_axis=0, concat_axis=0, tiled=True)

    def add_owned(kept, came):
        total = kept.astype(F32)
        for part in came:
            total = total + part.astype(F32)
        return total.astype(BF16)

    cross, first_pairs, second_pairs = [], [], []
    for half in range(2):
        for chip in range(lay.chips):
            source = (half * lay.chips + chip) * 2 + half
            peer = ((1 - half) * lay.chips + chip) * 2 + half
            head_block = half * lay.chips + chip
            cross.append((peer, source))
            first_pairs.append((source, 2 * head_block))
            second_pairs.append((source, 2 * head_block + 1))

    def out_split(values):
        values = values.reshape(2, lay.wsh, out_rows, model)
        kept = pick(values, lay.wplace, 1)
        away = [pick(values, (lay.wplace + d) % lay.wsh, 1) for d in range(1, lay.wsh)]
        return kept, [lay.wsh_shift(a, d + 1) for d, a in enumerate(away)]

    def over_groups(values):
        parts = []
        for bits in range(lay.wsh):
            moved = values
            if bits:
                pairs = [(i, i ^ bits) for i in range(lay.wsh)]
                moved = lax.ppermute(values, "wsh", pairs)
            both = []
            for i in range(lay.wsh):
                both += [(i, lay.wsh + (i ^ bits)), (lay.wsh + i, i ^ bits)]
            parts += [moved, lax.ppermute(values, ("half", "wsh"), both)]
        return parts

    project_step(0)
    forward_step(0)
    project_step(1, (edges[0],))
    forward_step(1)
    out_pieces, mixed[1] = join(out_pieces, mixed[1])
    w_out = own_rows(*out_pieces)
    own = stats_step(0)
    parts = team_parts(own, lay)
    own1 = stats_step(1, (own,))
    sums = add_all(parts)
    d_mixed0, out, gain0 = back_step(0, sums, (own1,))
    out0 = team_sum(out)
    d_mixed1, out, gain1 = back_step(1, add_all(team_parts(own1, lay)), (gain0,))
    out1 = team_sum(out)
    flat_gates = [d.reshape(length, inner) for d in d_gates]
    gate_grad = row_grad(
        [(turned_normed[0], flat_gates[0]), (turned_normed[1], flat_gates[1])], BF16
    )
    gate_kept, gate_came = owned_parts(gate_grad)
    out_grad = out_grad_part(turned_gated, grad_near, grad_far, wait=(gate_kept,))
    out_kept, out_came = out_split(out_grad)
    scan_step(0, d_mixed0, (out_kept,))
    part, norm_gain0 = norm_step(0)
    gate_came, out_came, d_mixed1, part = join(gate_came, out_came, d_mixed1, part)
    norm0 = team_sum(part)
    by_gate = to_owners(add_owned(gate_kept, gate_came))
    out_kept = add_owned(out_kept, out_came)
    out_came = lax.ppermute(out_kept, ALL, cross)
    sum0 = two_halves(out0, lay)
    scan_step(1, d_mixed1)
    part, norm_gain1 = norm_step(1)
    scan_grad = row_grad(
        [(turned_normed[0], d_raws[0]), (turned_normed[1], d_raws[1])], BF16, wait=(norm_gain1,)
    )
    scan_kept, scan_came = owned_parts(scan_grad)
    by_gate, out_came, sum0, scan_kept, part = join(by_gate, out_came, sum0, scan_kept, part)
    norm1 = team_sum(part)
    out_held = (out_kept.astype(F32) + out_came.astype(F32)).astype(BF16)
    out_first = lax.ppermute(out_held[0], ALL, first_pairs)
    out_second = lax.ppermute(out_held[1], ALL, second_pairs)
    small = over_groups(own_small(norm_gain1))
    scan_came, sum1, norm0, small = join(
        scan_came, two_halves(out1, lay), two_halves(norm0, lay), small
    )
    by_scan = to_owners(add_owned(scan_kept, scan_came))
    small = team_parts(pack_small(add_all(small)), lay)
    by_scan, norm1, small = join(by_scan, two_halves(norm1, lay), small)
    small = add_all(small)
    out_proj_grad = out_first.astype(F32) + out_second.astype(F32)

    def whole_place(first, second):
        mine = jnp.stack([first[0], second[0]], 0)
        other = jnp.stack([first[1], second[1]], 0)
        return both_halves(mine, other, lay)

    block_out = (hidden_wide + whole_place(sum0, sum1).astype(F32)).astype(BF16)

    def hidden_step():
        d_scaled = whole_place(norm0, norm1).astype(F32) * norm_gain
        inward = jnp.mean(d_scaled * hidden_wide, axis=-1, keepdims=True)
        return (
            cotangent.astype(F32)
            + norm_scale * d_scaled
            - hidden_wide * (norm_scale * norm_scale * norm_scale * inward)
        )

    hidden_grad = hidden_step()

    order = [(b % lay.chips) * 2 + b // lay.chips for b in range(team)]

    def by_member_parts(parts):
        return parts.reshape(2, team, in_rows, parts.shape[-1])

    in_proj_grad = owned_rows(order, by_member_parts(by_gate), by_member_parts(by_scan))
    ngain_all, conv_all, cbias_all, shift_all, rate_all, skip_all, ggain_all = unpack_small(small)
    return (
        block_out,
        hidden_grad,
        ngain_all,
        in_proj_grad,
        conv_all,
        cbias_all,
        shift_all,
        rate_all,
        skip_all,
        ggain_all,
        out_proj_grad,
    )


def solution(mesh):
    parts, wsh = mesh.devices.shape
    fine = Mesh(mesh.devices.reshape(2, parts // 4, 2, wsh), ("half", "chip", "core", "wsh"))
    by_token = P("wsh", ALL, None)
    by_row = P("wsh", None)
    owned = P(ALL + ("wsh",), None)
    whole = P()
    return jax.shard_map(
        shards,
        mesh=fine,
        in_specs=(by_token, by_token, whole, by_row) + (whole,) * 6 + (by_row,),
        out_specs=(by_token, by_token, whole, owned) + (whole,) * 6 + (owned,),
        check_vma=False,
    )
```

```python
import functools
import jax
import jax.numpy as jnp
from jax import lax
from jax.experimental import pallas as pl
from jax.experimental.pallas import tpu as pltpu
from jax.sharding import Mesh
from jax.sharding import PartitionSpec as P

STATE = 128
HEADDIM = 64
SPAN = 256
INNER = 4096
EPS = 1e-05
HIGH = lax.Precision.HIGHEST
NEG = -1e30
F32 = jnp.float32
BF16 = jnp.bfloat16


def dot_plain(left, right, precision=None):
    return lax.dot_general(
        left, right, (((1,), (0,)), ((), ())), preferred_element_type=F32, precision=precision
    )


def dot_lanes(left, right):
    return lax.dot_general(left, right, (((1,), (1,)), ((), ())), preferred_element_type=F32)


def dot_rows(left, right):
    return lax.dot_general(left, right, (((0,), (0,)), ((), ())), preferred_element_type=F32)


def softplus(values):
    return jnp.maximum(values, 0.0) + jnp.log1p(jnp.exp(-jnp.abs(values)))


def sigmoid(values):
    return 1.0 / (1.0 + jnp.exp(-values))


def head_rows(raw_steps, shift, neg_rate):
    span, heads = raw_steps.shape
    wide = jnp.concatenate([raw_steps, jnp.zeros((span, 128 - heads), F32)], 1)
    raw = wide.T[:heads] + shift
    step = softplus(raw)
    order = lax.broadcasted_iota(jnp.int32, (span, span), 0)
    until = lax.broadcasted_iota(jnp.int32, (span, span), 1)
    upper = jnp.where(order <= until, 1.0, 0.0)
    cum = dot_plain(step * neg_rate, upper, HIGH)
    last = cum[:, span - 1 :]
    return raw, step, cum, jnp.exp(cum), jnp.exp(last - cum)


def as_columns(rows):
    count, span = rows.shape
    return jnp.concatenate([rows, jnp.zeros((128 - count, span), F32)], 0).T


def spread_lanes(columns, start, heads):
    span = columns.shape[0]
    low = lax.broadcasted_iota(jnp.int32, (span, 2 * HEADDIM), 1) < HEADDIM
    pieces = []
    for pair in range(heads // 2):
        at = start + 2 * pair
        pieces.append(jnp.where(low, columns[:, at : at + 1], columns[:, at + 1 : at + 2]))
    return jnp.concatenate(pieces, 1)


def pair_halves(values, pair):
    slab = values[:, 2 * HEADDIM * pair : 2 * HEADDIM * (pair + 1)]
    low = lax.broadcasted_iota(jnp.int32, slab.shape, 1) < HEADDIM
    zero = jnp.zeros_like(slab)
    return slab, (jnp.where(low, slab, zero), jnp.where(low, zero, slab))


def convolve(window, taps, offset, span):
    running = None
    for k in range(taps.shape[0]):
        term = window[pl.ds(offset(k), span), :] * taps[k : k + 1, :]
        running = term if running is None else running + term
    return running


def scan_forward_body(
    heads,
    half_ref,
    raw_ref,
    taps_ref,
    bias_ref,
    shift_ref,
    rate_ref,
    skip_ref,
    mixed_ref,
    start_ref,
    edge_ref,
    state,
    window,
):
    span = raw_ref.shape[0]
    inner = heads * HEADDIM
    wide = inner + 2 * STATE
    first = pl.program_id(1) == 0

    @pl.when(first)
    def _():
        state[...] = jnp.zeros_like(state)
        window[0:8, :] = jnp.zeros((8, wide), F32)

    @pl.when(jnp.logical_not(first))
    def _():
        window[0:8, :] = window[span : span + 8, :]

    edge_ref[...] = window[0:8, :]
    window[8 : 8 + span, :] = raw_ref[:, :wide].astype(F32)
    conv = convolve(window, taps_ref[...], lambda k: 5 + k, span) + bias_ref[...]
    act = conv * sigmoid(conv)
    x_act = act[:, :inner]
    b_low = act[:, inner : inner + STATE].astype(BF16)
    c_act = act[:, inner + STATE :]
    c_low = c_act.astype(BF16)
    c_both = jnp.concatenate([c_low, (c_act - c_low.astype(F32)).astype(BF16)], 1)
    raw, step, cum, grown, tail = head_rows(
        raw_ref[:, wide:].astype(F32), shift_ref[...], -jnp.exp(rate_ref[...])
    )
    columns = as_columns(jnp.concatenate([cum, step, grown, tail], 0))
    step_wide = spread_lanes(columns, heads, heads)
    grown_wide = spread_lanes(columns, 2 * heads, heads)
    tail_wide = spread_lanes(columns, 3 * heads, heads)
    stepped = x_act * step_wide
    stepped_low = stepped.astype(BF16)
    held = state[...]
    start_ref[...] = held
    held_low = held.astype(BF16)
    scores = dot_lanes(c_both, jnp.concatenate([b_low, b_low], 1))
    carried = dot_plain(c_both, jnp.concatenate([held_low, held_low], 0)) * grown_wide
    carried = carried + skip_ref[...] * x_act
    rows = lax.broadcasted_iota(jnp.int32, (span, span), 0)
    cols = lax.broadcasted_iota(jnp.int32, (span, span), 1)
    causal = rows >= cols
    for pair in range(heads // 2):
        _, halves = pair_halves(stepped_low, pair)
        total = carried[:, 2 * HEADDIM * pair : 2 * HEADDIM * (pair + 1)]
        for half in range(2):
            head = 2 * pair + half
            spread = columns[:, head : head + 1] - cum[head : head + 1, :]
            weights = jnp.exp(jnp.where(causal, spread, NEG)) * scores
            total = total + dot_plain(weights.astype(BF16), halves[half])
        mixed_ref[:, 2 * HEADDIM * pair : 2 * HEADDIM * (pair + 1)] = total.astype(BF16)
    fresh = dot_rows(b_low, (stepped * tail_wide).astype(BF16))
    state[...] = held * grown_wide[span - 1 : span, :] + fresh


def scan_forward(half, raw, at, taps, bias, shift, log_rate, skip_wide, wait=()):
    _, length, width = raw.shape
    seqs = 1
    heads = shift.shape[0]
    inner = heads * HEADDIM
    wide = inner + 2 * STATE
    spans = length // SPAN
    whole = lambda shape: pl.BlockSpec(shape, lambda s, i, t: (0,) * len(shape))
    lies = lambda i, t: (i + t[0] * (spans // 2)) % spans
    return call_after(
        wait,
        functools.partial(scan_forward_body, heads),
        (half, raw, taps, bias, shift, log_rate, skip_wide),
        scalars=1,
        grid=(seqs, spans),
        in_specs=[
            pl.BlockSpec((None, SPAN, width), lambda s, i, t: (at, lies(i, t), 0)),
            whole(taps.shape),
            whole(bias.shape),
            whole(shift.shape),
            whole(log_rate.shape),
            whole(skip_wide.shape),
        ],
        out_specs=[
            pl.BlockSpec((None, SPAN, inner), lambda s, i, t: (s, lies(i, t), 0)),
            pl.BlockSpec((None, None, STATE, inner), lambda s, i, t: (s, i, 0, 0)),
            pl.BlockSpec((None, None, 8, wide), lambda s, i, t: (s, i, 0, 0)),
        ],
        out_shape=[
            jax.ShapeDtypeStruct((seqs, length, inner), BF16),
            jax.ShapeDtypeStruct((seqs, spans, STATE, inner), F32),
            jax.ShapeDtypeStruct((seqs, spans, 8, wide), F32),
        ],
        scratch_shapes=[pltpu.VMEM((STATE, inner), F32), pltpu.VMEM((SPAN + 8, wide), F32)],
        compiler_params=kernel_params(),
        cost_estimate=light_cost(10),
        name="scan_forward",
    )


def scan_backward_body(
    heads,
    half_ref,
    raw_ref,
    down_ref,
    start_ref,
    edge_ref,
    taps_ref,
    bias_ref,
    shift_ref,
    rate_ref,
    skip_ref,
    draw_ref,
    dtaps_ref,
    dskip_ref,
    dhead_ref,
    dstate,
    window,
    ahead,
):
    span = raw_ref.shape[0]
    inner = heads * HEADDIM
    wide = inner + 2 * STATE
    step_at = pl.program_id(1)

    @pl.when((pl.program_id(0) == 0) & (step_at == 0))
    def _():
        dtaps_ref[...] = jnp.zeros_like(dtaps_ref)
        dskip_ref[...] = jnp.zeros_like(dskip_ref)
        dhead_ref[...] = jnp.zeros_like(dhead_ref)

    @pl.when(step_at == 0)
    def _():
        dstate[...] = jnp.zeros_like(dstate)
        ahead[span : span + 8, :] = jnp.zeros((8, wide), F32)

    @pl.when(step_at != 0)
    def _():
        ahead[span : span + 8, :] = ahead[0:8, :]

    taps = taps_ref[...]
    window[0:8, :] = edge_ref[...]
    window[8 : 8 + span, :] = raw_ref[:, :wide].astype(F32)
    conv = convolve(window, taps, lambda k: 5 + k, span) + bias_ref[...]
    sig = sigmoid(conv)
    act = conv * sig
    x_act = act[:, :inner]
    b_low = act[:, inner : inner + STATE].astype(BF16)
    c_low = act[:, inner + STATE :].astype(BF16)
    neg_rate = -jnp.exp(rate_ref[...])
    raw, step, cum, grown, tail = head_rows(raw_ref[:, wide:].astype(F32), shift_ref[...], neg_rate)
    columns = as_columns(jnp.concatenate([cum, step, grown, tail], 0))
    step_wide = spread_lanes(columns, heads, heads)
    grown_wide = spread_lanes(columns, 2 * heads, heads)
    tail_wide = spread_lanes(columns, 3 * heads, heads)
    stepped = x_act * step_wide
    stepped_low = stepped.astype(BF16)
    down_low = down_ref[...]
    down = down_low.astype(F32)
    held = start_ref[...]
    held_low = held.astype(BF16)
    dheld = dstate[...]
    dheld_low = dheld.astype(BF16)
    scores = dot_lanes(b_low, c_low)
    rows = lax.broadcasted_iota(jnp.int32, (span, span), 0)
    cols = lax.broadcasted_iota(jnp.int32, (span, span), 1)
    causal = cols >= rows
    dscores = jnp.zeros((span, span), F32)
    dstepped_parts = []
    gained = []
    lost = []
    for pair in range(heads // 2):
        _, x_halves = pair_halves(stepped_low, pair)
        down_pair, down_halves = pair_halves(down_low, pair)
        total = jnp.zeros((span, 2 * HEADDIM), F32)
        for half in range(2):
            head = 2 * pair + half
            spread = cum[head : head + 1, :] - columns[:, head : head + 1]
            decay = jnp.exp(jnp.where(causal, spread, NEG))
            weights = decay * scores
            dweights = dot_lanes(x_halves[half], down_pair)
            dscores = dscores + decay * dweights
            both = weights * dweights
            gained.append(jnp.sum(both, axis=0, keepdims=True))
            lost.append(jnp.sum(both, axis=1, keepdims=True))
            total = total + dot_plain(weights.astype(BF16), down_halves[half])
        dstepped_parts.append(total)
    dscores_low = dscores.astype(BF16)
    dtail = dot_plain(b_low, dheld_low) * tail_wide
    dstepped = jnp.concatenate(dstepped_parts, 1) + dtail
    down_grown = (down * grown_wide).astype(BF16)
    d_b = dot_plain(dscores_low, c_low) + dot_lanes((stepped * tail_wide).astype(BF16), dheld_low)
    d_c = dot_rows(dscores_low, b_low) + dot_lanes(down_grown, held_low)
    carried = dot_plain(c_low, held_low) * grown_wide
    member = lax.broadcasted_iota(jnp.int32, (heads, inner), 1) // HEADDIM
    which = lax.broadcasted_iota(jnp.int32, (heads, inner), 0)
    pick = jnp.where(member == which, 1.0, 0.0)
    pick_low = pick.astype(BF16)
    carried_sum = dot_lanes(pick_low, (down * carried).astype(BF16))
    tail_sum = dot_lanes(pick_low, (stepped * dtail).astype(BF16))
    step_sum = dot_lanes(pick_low, (x_act * dstepped).astype(BF16))
    lost_rows = as_columns_back(jnp.concatenate(lost, 1))
    state_sum = jnp.sum(pick * jnp.sum(held * dheld, axis=0, keepdims=True), axis=1, keepdims=True)
    dcum = jnp.concatenate(gained, 0) + carried_sum - lost_rows - tail_sum
    since = jnp.where(rows >= cols, 1.0, 0.0)
    whole_part = jnp.sum(tail_sum, axis=1, keepdims=True) + grown[:, span - 1 :] * state_sum
    dlog = dot_plain(dcum, since, HIGH) + whole_part
    draw_step = (step_sum + neg_rate * dlog) * sigmoid(raw)
    dhead_ref[0] += neg_rate * jnp.sum(step * dlog, axis=1, keepdims=True)
    dhead_ref[1] += jnp.sum(draw_step, axis=1, keepdims=True)
    dskip_ref[...] += jnp.sum(down * x_act, axis=0, keepdims=True)
    d_x = dstepped * step_wide + skip_ref[...] * down
    dconv = jnp.concatenate([d_x, d_b, d_c], 1) * (sig * (1.0 + conv * (1.0 - sig)))
    ahead[0:span, :] = dconv
    draw = convolve(ahead, taps, lambda k: 3 - k, span)
    draw_ref[:, :wide] = draw.astype(BF16)
    draw_ref[:, wide:] = as_columns(draw_step)[:, :heads].astype(BF16)
    for k in range(taps.shape[0]):
        dtaps_ref[k : k + 1, :] += jnp.sum(
            dconv * window[pl.ds(5 + k, span), :], axis=0, keepdims=True
        )
    dtaps_ref[4:5, :] += jnp.sum(dconv, axis=0, keepdims=True)
    dstate[...] = dheld * grown_wide[span - 1 : span, :] + dot_rows(c_low, down_grown)


def as_columns_back(columns):
    span, heads = columns.shape
    return jnp.concatenate([columns, jnp.zeros((span, 128 - heads), F32)], 1).T[:heads]


def scan_backward(half, raw, at, down, starts, edges, taps, bias, shift, log_rate, skip_wide, wait=()):
    _, length, width = raw.shape
    seqs = 1
    heads = shift.shape[0]
    inner = heads * HEADDIM
    wide = inner + 2 * STATE
    spans = length // SPAN
    whole = lambda shape: pl.BlockSpec(shape, lambda s, i, t: (0,) * len(shape))
    lies = lambda i, t: (spans - 1 - i + t[0] * (spans // 2)) % spans
    turned = lambda s, i, t: (s, lies(i, t), 0)
    return call_after(
        wait,
        functools.partial(scan_backward_body, heads),
        (half, raw, down, starts, edges, taps, bias, shift, log_rate, skip_wide),
        scalars=1,
        grid=(seqs, spans),
        in_specs=[
            pl.BlockSpec((None, SPAN, width), lambda s, i, t: (at, lies(i, t), 0)),
            pl.BlockSpec((None, SPAN, inner), turned),
            pl.BlockSpec((None, None, STATE, inner), lambda s, i, t: (s, spans - 1 - i, 0, 0)),
            pl.BlockSpec((None, None, 8, wide), lambda s, i, t: (s, spans - 1 - i, 0, 0)),
            whole(taps.shape),
            whole(bias.shape),
            whole(shift.shape),
            whole(log_rate.shape),
            whole(skip_wide.shape),
        ],
        out_specs=[
            pl.BlockSpec((None, SPAN, width), turned),
            whole((8, wide)),
            whole((1, inner)),
            whole((2, heads, 1)),
        ],
        out_shape=[
            jax.ShapeDtypeStruct((seqs, length, width), BF16),
            jax.ShapeDtypeStruct((8, wide), F32),
            jax.ShapeDtypeStruct((1, inner), F32),
            jax.ShapeDtypeStruct((2, heads, 1), F32),
        ],
        scratch_shapes=[
            pltpu.VMEM((STATE, inner), F32),
            pltpu.VMEM((SPAN + 8, wide), F32),
            pltpu.VMEM((SPAN + 8, wide), F32),
        ],
        compiler_params=kernel_params(),
        cost_estimate=light_cost(22),
        name="scan_backward",
    )

def kernel_params():
    return pltpu.CompilerParams(vmem_limit_bytes=58 * 1024 * 1024)


def call_after(wait, body, values, in_specs, scalars=0, **rest):
    held = [pl.BlockSpec(memory_space=pl.ANY)] * len(wait)

    def inner_body(*refs):
        body(*refs[: len(values)], *refs[len(values) + len(wait) :])

    if scalars:
        rest["grid_spec"] = pltpu.PrefetchScalarGridSpec(
            num_scalar_prefetch=scalars,
            grid=rest.pop("grid"),
            in_specs=list(in_specs) + held,
            out_specs=rest.pop("out_specs"),
            scratch_shapes=rest.pop("scratch_shapes"),
        )
    else:
        rest["in_specs"] = list(in_specs) + held
    return pl.pallas_call(inner_body, **rest)(*values, *wait)


def light_cost(micros):
    work = int(micros * 1e9 * 1.0)
    return pl.CostEstimate(flops=work, bytes_accessed=work // 400, transcendentals=0)


def both_parts(near_ref, far_ref):
    return jnp.concatenate(
        [ref[member] for member in range(near_ref.shape[0]) for ref in (near_ref, far_ref)], 0
    )


def gathered(values, at):
    _, _, tokens, width = values.shape
    return pl.BlockSpec((2, None, tokens, width), lambda i: (i, at, 0, 0))


def project_body(inner, near_ref, far_ref, weight_ref, gate_ref, raw_ref, turned_ref):
    values = both_parts(near_ref, far_ref)
    put_by_member(gate_ref, dot_lanes(values, weight_ref[:inner, :]))
    put_by_member(raw_ref, dot_lanes(values, weight_ref[inner:, :]))
    for half, ref in enumerate((near_ref, far_ref)):
        turned_ref[half] = jnp.concatenate([ref[0], ref[1]], 0).T


def project_tokens(near, far, at, weight, inner, wait=()):
    team, _, tokens, model = near.shape
    width = weight.shape[0]

    def halves(size):
        return pl.BlockSpec((2, 2, tokens, size), lambda i: (0, i, 0, 0))

    return call_after(
        wait,
        functools.partial(project_body, inner),
        (near, far, weight),
        grid=(team // 2,),
        in_specs=[
            gathered(near, at),
            gathered(far, at),
            pl.BlockSpec((width, model), lambda i: (0, 0)),
        ],
        out_specs=[
            halves(inner),
            halves(width - inner),
            pl.BlockSpec((2, model, 2 * tokens), lambda i: (0, 0, i)),
        ],
        out_shape=[
            jax.ShapeDtypeStruct((2, team, tokens, inner), BF16),
            jax.ShapeDtypeStruct((2, team, tokens, width - inner), BF16),
            jax.ShapeDtypeStruct((2, model, team * tokens), BF16),
        ],
        compiler_params=kernel_params(),
        cost_estimate=light_cost(11),
        name="project_tokens",
    )


def by_member(ref):
    return jnp.concatenate(
        [ref[half, member] for member in range(ref.shape[1]) for half in range(2)], 0
    )


def put_by_member(ref, rows):
    tokens = ref.shape[2]
    for member in range(ref.shape[1]):
        for half in range(2):
            at = (member * 2 + half) * tokens
            ref[half, member] = rows[at : at + tokens].astype(ref.dtype)


def gate_stats_body(near_ref, far_ref, weight_ref, mixed_ref, gate_ref, gain_ref, down_ref, sums_ref):
    d_gated = dot_lanes(both_parts(near_ref, far_ref), weight_ref[...])
    gate = by_member(gate_ref).astype(F32)
    unit = by_member(mixed_ref).astype(F32) * gate * sigmoid(gate)
    put_by_member(down_ref, d_gated)
    square = jnp.sum(unit * unit, axis=1, keepdims=True)
    cross = jnp.sum(d_gated * gain_ref[...] * unit, axis=1, keepdims=True)
    sums_ref[...] = as_columns_back(jnp.concatenate([square, cross], 1))


def gate_stats(near, near_at, far, far_at, weight, mixed, gate, gain, wait=()):
    team, _, tokens, model = near.shape
    inner = weight.shape[0]
    pair = 2
    rows = pair * 2 * tokens
    natural = pl.BlockSpec((2, pair, tokens, inner), lambda i: (0, i, 0, 0))
    return call_after(
        wait,
        gate_stats_body,
        (near, far, weight, mixed, gate, gain),
        grid=(team // pair,),
        in_specs=[
            gathered(near, near_at),
            gathered(far, far_at),
            pl.BlockSpec((inner, model), lambda i: (0, 0)),
            natural,
            natural,
            pl.BlockSpec((1, inner), lambda i: (0, 0)),
        ],
        out_specs=[
            natural,
            pl.BlockSpec((2, rows), lambda i: (0, i)),
        ],
        out_shape=[
            jax.ShapeDtypeStruct((2, team, tokens, inner), F32),
            jax.ShapeDtypeStruct((2, team * 2 * tokens), F32),
        ],
        compiler_params=kernel_params(),
        cost_estimate=light_cost(7),
        name="gate_stats",
    )


def gate_back_body(
    mixed_ref,
    gate_ref,
    down_ref,
    sums_ref,
    gain_ref,
    weight_ref,
    turned_ref,
    d_mixed_ref,
    d_gate_ref,
    out_ref,
    d_gain_ref,
):
    @pl.when(pl.program_id(0) == 0)
    def _():
        d_gain_ref[...] = jnp.zeros_like(d_gain_ref)

    columns = as_columns(sums_ref[...])
    gain = gain_ref[...]
    scale = lax.rsqrt(columns[:, 0:1] / INNER + EPS)
    pull = columns[:, 1:2] * (scale * scale * scale / INNER)
    mixed = by_member(mixed_ref).astype(F32)
    gate = by_member(gate_ref).astype(F32)
    down = by_member(down_ref)
    sig = sigmoid(gate)
    act = gate * sig
    unit = mixed * act
    scaled = unit * scale
    gated_wide = scaled * gain
    tokens = mixed_ref.shape[2]
    for half in range(2):
        rows = [gated_wide[(2 * m + half) * tokens : (2 * m + half + 1) * tokens] for m in range(2)]
        turned_ref[half] = jnp.concatenate(rows, 0).T.astype(BF16)
    out_ref[...] = dot_plain(gated_wide.astype(BF16), weight_ref[...]).astype(BF16)
    d_unit = down * gain * scale - unit * pull
    put_by_member(d_mixed_ref, d_unit * act)
    put_by_member(d_gate_ref, d_unit * mixed * (sig * (1.0 + gate * (1.0 - sig))))
    d_gain_ref[...] += jnp.sum(down * scaled, axis=0, keepdims=True)


def gate_back(mixed, gate, down, sums, gain, weight, wait=()):
    _, team, tokens, inner = down.shape
    model = weight.shape[1]
    rows = 4 * tokens
    natural = pl.BlockSpec((2, 2, tokens, inner), lambda i: (0, i, 0, 0))
    one = pl.BlockSpec((1, inner), lambda i: (0, 0))
    return call_after(
        wait,
        gate_back_body,
        (mixed, gate, down, sums, gain, weight),
        grid=(team // 2,),
        in_specs=[
            natural,
            natural,
            natural,
            pl.BlockSpec((2, rows), lambda i: (0, i)),
            one,
            pl.BlockSpec((inner, model), lambda i: (0, 0)),
        ],
        out_specs=[
            pl.BlockSpec((2, inner, 2 * tokens), lambda i: (0, 0, i)),
            natural,
            natural,
            pl.BlockSpec((rows, model), lambda i: (i, 0)),
            one,
        ],
        out_shape=[
            jax.ShapeDtypeStruct((2, inner, team * tokens), BF16),
            jax.ShapeDtypeStruct((2, team, tokens, inner), BF16),
            jax.ShapeDtypeStruct((2, team, tokens, inner), BF16),
            jax.ShapeDtypeStruct((team * 2 * tokens, model), BF16),
            jax.ShapeDtypeStruct((1, inner), F32),
        ],
        compiler_params=kernel_params(),
        cost_estimate=light_cost(0),
        name="gate_back",
    )


def row_grad_body(pairs, cols, has_base, *refs):
    out_ref = refs[-1]
    total = None
    for k in range(pairs):
        left_ref = refs[2 * k]
        right_ref = refs[2 * k + 1]
        count, _, depth = left_ref.shape
        for part in range(count):
            right = right_ref[part * depth : (part + 1) * depth, :]
            if cols is not None:
                right = right[:, cols[0] : cols[1]]
            term = dot_plain(left_ref[part], right)
            total = term if total is None else total + term
    if has_base:
        base = refs[2 * pairs][...]
        if cols is not None:
            base = base[:, cols[0] : cols[1]]
        total = total + base
    out_ref[...] = total.astype(out_ref.dtype)


def row_grad(operands, kind, cols=None, base=None, wait=()):
    rows = operands[0][0].shape[1]
    width = operands[0][1].shape[1]
    got = width if cols is None else cols[1] - cols[0]
    tile = min(512, rows)
    if got > 1024:
        tile = min(256, rows)
    specs, args = [], []
    for left, right in operands:
        specs.append(pl.BlockSpec((left.shape[0], tile, left.shape[2]), lambda i: (0, i, 0)))
        specs.append(pl.BlockSpec(right.shape, lambda i: (0, 0)))
        args += [left, right]
    if base is not None:
        specs.append(pl.BlockSpec((tile, width), lambda i: (i, 0)))
        args.append(base)
    return call_after(
        wait,
        functools.partial(row_grad_body, len(operands), cols, base is not None),
        tuple(args),
        grid=(rows // tile,),
        in_specs=specs,
        out_specs=pl.BlockSpec((tile, got), lambda i: (i, 0)),
        out_shape=jax.ShapeDtypeStruct((rows, got), kind),
        compiler_params=kernel_params(),
        cost_estimate=light_cost(0),
        name="row_grad",
    )


def norm_part_body(d_gate_ref, d_raw_ref, near_ref, far_ref, weight_ref, out_ref, gain_ref):
    @pl.when(pl.program_id(0) == 0)
    def _():
        gain_ref[...] = jnp.zeros_like(gain_ref)

    inner = d_gate_ref.shape[-1]
    part = dot_plain(by_member(d_gate_ref), weight_ref[:inner, :])
    part = part + dot_plain(by_member(d_raw_ref), weight_ref[inner:, :])
    normed = both_parts(near_ref, far_ref).astype(F32)
    gain_ref[...] += jnp.sum(part * normed, axis=0, keepdims=True)
    out_ref[...] = part.astype(BF16)


def norm_part(d_gate, d_raw, near, far, at, weight, wait=()):
    _, team, tokens, inner = d_gate.shape
    width = d_raw.shape[-1]
    model = weight.shape[1]
    rows = 4 * tokens

    def natural(size):
        return pl.BlockSpec((2, 2, tokens, size), lambda i: (0, i, 0, 0))

    return call_after(
        wait,
        norm_part_body,
        (d_gate, d_raw, near, far, weight),
        grid=(team // 2,),
        in_specs=[
            natural(inner),
            natural(width),
            gathered(near, at),
            gathered(far, at),
            pl.BlockSpec((inner + width, model), lambda i: (0, 0)),
        ],
        out_specs=[
            pl.BlockSpec((rows, model), lambda i: (i, 0)),
            pl.BlockSpec((1, model), lambda i: (0, 0)),
        ],
        out_shape=[
            jax.ShapeDtypeStruct((team * 2 * tokens, model), BF16),
            jax.ShapeDtypeStruct((1, model), F32),
        ],
        compiler_params=kernel_params(),
        cost_estimate=light_cost(0),
        name="norm_part",
    )


def out_grad_body(seqs, *refs):
    lefts = refs[:seqs]
    near_ref, far_ref, out_ref = refs[seqs:]
    depth = lefts[0].shape[2]
    tile = out_ref.shape[1]
    total = None
    for s in range(seqs):
        for half, ref in enumerate((near_ref, far_ref)):
            term = dot_plain(lefts[s][half], ref[:, s].reshape(depth, tile))
            total = term if total is None else total + term
    out_ref[...] = total.astype(out_ref.dtype)


def out_grad_part(lefts, near, far, wait=()):
    team, seqs, tokens, model = near.shape
    inner = lefts[0].shape[1]
    tile = 256
    part = pl.BlockSpec((team, seqs, tokens, tile), lambda i: (0, 0, 0, i))
    return call_after(
        wait,
        functools.partial(out_grad_body, seqs),
        (*lefts, near, far),
        grid=(model // tile,),
        in_specs=[pl.BlockSpec(left.shape, lambda i: (0, 0, 0)) for left in lefts] + [part, part],
        out_specs=pl.BlockSpec((inner, tile), lambda i: (0, i)),
        out_shape=jax.ShapeDtypeStruct((inner, model), BF16),
        compiler_params=kernel_params(),
        cost_estimate=light_cost(8),
        name="out_grad_part",
    )


def owned_rows_body(order, inner, gate_ref, scan_ref, out_ref):
    team = len(order)
    width = scan_ref.shape[-1]
    steps = width - inner - 2 * STATE
    shared = None
    for place, member in enumerate(order):
        gate = gate_ref[0, member].astype(F32) + gate_ref[1, member].astype(F32)
        scan = scan_ref[0, member].astype(F32) + scan_ref[1, member].astype(F32)
        out_ref[:, place * inner : (place + 1) * inner] = gate
        out_ref[:, (team + place) * inner : (team + place + 1) * inner] = scan[:, :inner]
        term = scan[:, inner : inner + 2 * STATE]
        shared = term if shared is None else shared + term
        at = 2 * team * inner + 2 * STATE + place * steps
        out_ref[:, at : at + steps] = scan[:, inner + 2 * STATE :]
    out_ref[:, 2 * team * inner : 2 * team * inner + 2 * STATE] = shared


def owned_rows(order, gate, scan):
    _, team, rows, inner = gate.shape
    steps = scan.shape[-1] - inner - 2 * STATE
    total = team * (2 * inner + steps) + 2 * STATE
    return pl.pallas_call(
        functools.partial(owned_rows_body, order, inner),
        out_shape=jax.ShapeDtypeStruct((rows, total), F32),
        compiler_params=kernel_params(),
        cost_estimate=light_cost(3),
        name="owned_rows",
    )(gate, scan)


TEAM = ("chip", "core")
ALL = ("half", "chip", "core")
EVERY = ALL + ("wsh",)


def join(*values):
    leaves, tree = jax.tree.flatten(values)
    anywhere = [pl.BlockSpec(memory_space=pl.ANY)] * len(leaves)
    out = pl.pallas_call(
        lambda *refs: None,
        in_specs=anywhere,
        out_specs=anywhere,
        out_shape=[jax.ShapeDtypeStruct(v.shape, v.dtype) for v in leaves],
        input_output_aliases={k: k for k in range(len(leaves))},
        cost_estimate=light_cost(0),
        name="join",
    )(*leaves)
    return jax.tree.unflatten(tree, out)


class Layout:
    def __init__(self):
        self.chips = lax.axis_size("chip")
        self.wsh = lax.axis_size("wsh")
        self.team = 2 * self.chips
        self.parts = 2 * self.team
        self.half = lax.axis_index("half")
        self.chip = lax.axis_index("chip")
        self.core = lax.axis_index("core")
        self.wplace = lax.axis_index("wsh")
        self.member = self.chip * 2 + self.core
        self.block = self.core * self.chips + self.chip

    def other_core(self, values):
        return lax.ppermute(values, "core", [(0, 1), (1, 0)])

    def other_half(self, values):
        return lax.ppermute(values, "half", [(0, 1), (1, 0)])

    def chip_flip(self, values, bits):
        return lax.ppermute(values, "chip", [(i, i ^ bits) for i in range(self.chips)])

    def wsh_shift(self, values, shift):
        size = self.wsh
        return lax.ppermute(values, "wsh", [(i, (i + shift) % size) for i in range(size)])


def pick(values, at, axis):
    return lax.dynamic_index_in_dim(values, at, axis, keepdims=False)


def split_halves(own, lay):
    count = own.shape[0] // 2
    keep = lax.dynamic_slice_in_dim(own, lay.half * count, count, 0)
    away = lax.dynamic_slice_in_dim(own, (1 - lay.half) * count, count, 0)
    return keep, away


def team_gather(values):
    return lax.all_gather(values, TEAM, axis=0)


def both_halves(mine, other, lay):
    first = jnp.where(lay.half == 0, mine, other)
    second = jnp.where(lay.half == 0, other, mine)
    return jnp.concatenate([first, second], 0)


def team_sum(part):
    own = lax.psum_scatter(part, TEAM, scatter_dimension=0, tiled=True)
    return own.reshape(2, own.shape[0] // 2, own.shape[1])


def two_halves(own, lay):
    return own[0], lay.other_half(own[1])


def columns_in_place(local, came, lay):
    blocks = []
    for place in range(lay.wsh):
        block = local
        for shift, piece in enumerate(came):
            block = jnp.where((lay.wplace - shift - 1) % lay.wsh == place, piece, block)
        blocks.append(block)
    return jnp.concatenate(blocks, 1)


def team_parts(values, lay):
    values = values + lay.other_core(values)
    return [values] + [lay.chip_flip(values, bits) for bits in range(1, lay.chips)]


def add_all(parts):
    while len(parts) > 1:
        parts = [parts[k] + parts[k + 1] for k in range(0, len(parts), 2)]
    return parts[0]


def shards(
    hidden,
    cotangent,
    norm_gain,
    in_proj,
    conv_weight,
    conv_bias,
    dt_bias,
    a_log,
    d_skip,
    gate_gain,
    out_proj,
):
    lay = Layout()
    seqs, tokens, model = hidden.shape
    count = seqs // 2
    length = tokens * lay.parts
    inner = INNER // lay.team
    heads = inner // HEADDIM
    block = lay.block
    steps_at = 2 * INNER + 2 * STATE

    def columns(values, start, width, axis=1):
        return lax.dynamic_slice_in_dim(values, start, width, axis)

    hidden_wide = hidden.astype(F32)
    norm_scale = lax.rsqrt(jnp.mean(hidden_wide * hidden_wide, axis=-1, keepdims=True) + EPS)
    normed = (hidden_wide * norm_scale * norm_gain).astype(BF16)

    turned = in_proj.T
    local = jnp.concatenate(
        [
            columns(turned, block * inner, inner, 0),
            columns(turned, INNER + block * inner, inner, 0),
            turned[2 * INNER : steps_at],
            columns(turned, steps_at + block * heads, heads, 0),
        ],
        0,
    )

    def to_wsh(values):
        return [lay.wsh_shift(values, shift) for shift in range(1, lay.wsh)]

    cut = (inner // 128 + 1) * 128
    keep, away = split_halves(normed, lay)
    keep_grad, away_grad = split_halves(cotangent, lay)
    came_first, came, later, away_grad = join(
        to_wsh(local[:cut]), lay.other_half(away), local[cut:], away_grad
    )
    normed_near = team_gather(keep)
    normed_far = team_gather(came)
    rows_held = INNER // lay.wsh
    owner = (block * inner) // rows_held
    at_row = jnp.where(owner == lay.wplace, block * inner - owner * rows_held, 0)
    rows_here = columns(out_proj, at_row, inner, 0)
    came_last, came_grad, rows_here, normed_near = join(
        to_wsh(later), lay.other_half(away_grad), rows_here, normed_near
    )
    pieces = [jnp.concatenate(parts, 0) for parts in zip(came_first, came_last)]
    weight = columns_in_place(local, pieces, lay)
    out_pieces = []
    for shift in range(1, lay.wsh):
        pairs = []
        for place in range(lay.team):
            head_block = (place % 2) * lay.chips + place // 2
            holder = (head_block * inner) // rows_held
            source = place * lay.wsh + holder
            pairs.append((source, place * lay.wsh + (holder + shift) % lay.wsh))
        out_pieces.append(lax.ppermute(rows_here, TEAM + ("wsh",), pairs))

    def own_rows(first, *rest):
        total = jnp.where(owner == lay.wplace, rows_here, jnp.zeros_like(rows_here)) + first
        for piece in rest:
            total = total + piece
        return total

    taps = jnp.concatenate(
        [columns(conv_weight, block * inner, inner), conv_weight[:, INNER:]], 1
    )
    bias = jnp.concatenate([columns(conv_bias, block * inner, inner, 0), conv_bias[INNER:]], 0)
    shift_own = columns(dt_bias, block * heads, heads, 0)[:, None]
    rate_own = columns(a_log, block * heads, heads, 0)[:, None]
    skip_own = jnp.repeat(columns(d_skip, block * heads, heads, 0), HEADDIM)[None]
    gain_own = columns(gate_gain, block * inner, inner, 0)[None]
    params = (taps, bias[None], shift_own, rate_own, skip_own)
    normed_far, keep_grad, came_grad, weight, params, gain_own = join(
        normed_far, keep_grad, came_grad, weight, params, gain_own
    )
    grad_near = team_gather(keep_grad)
    grad_far = team_gather(came_grad)

    kernel = conv_weight.shape[0]
    shapes = [norm_gain.shape, conv_weight.shape, conv_bias.shape]
    shapes += [dt_bias.shape, a_log.shape, d_skip.shape, gate_gain.shape]

    def placed(values, width):
        full = jnp.zeros(values.shape[:-1] + (width,), F32)
        return lax.dynamic_update_slice_in_dim(
            full, values, block * values.shape[-1], values.ndim - 1
        )

    def own_small(norm_gain1):
        d_taps, d_skip_wide, d_head = jax.tree.map(lambda *v: sum(v[1:], v[0]), *small_scan)
        parts = [
            (norm_gain0 + norm_gain1)[0] / norm_gain,
            d_taps[: kernel + 1],
            d_head[:, :, 0],
            d_skip_wide.reshape(heads, HEADDIM).sum(1),
            (gain0 + gain1)[0],
        ]
        return jnp.concatenate([p.reshape(-1) for p in parts])

    def pack_small(own):
        sizes = [model, (kernel + 1) * (inner + 2 * STATE), 2 * heads, heads, inner]
        pieces, at = [], 0
        for size in sizes:
            pieces.append(own[at : at + size])
            at += size
        gain, d_taps, d_head, d_skip, d_gain = pieces
        d_taps = d_taps.reshape(kernel + 1, inner + 2 * STATE)
        d_taps = jnp.concatenate([placed(d_taps[:, :inner], INNER), d_taps[:, inner:]], 1)
        d_head = placed(d_head.reshape(2, heads), dt_bias.shape[0])
        small = [
            gain,
            d_taps[:kernel],
            d_taps[kernel],
            d_head[1],
            d_head[0],
            placed(d_skip, dt_bias.shape[0]),
            placed(d_gain, INNER),
        ]
        return jnp.concatenate([s.reshape(-1) for s in small])

    def unpack_small(packed):
        summed, at = [], 0
        for shape in shapes:
            size = 1
            for extent in shape:
                size *= extent
            summed.append(packed[at : at + size].reshape(shape))
            at += size
        return summed

    team = lay.team
    natural = (2, team, tokens)
    half_at = lay.half[None].astype(jnp.int32)
    out_rows = INNER // (lay.parts * lay.wsh)
    in_rows = model // (lay.parts * lay.wsh)

    gates, raws, turned_normed = [], [], []
    mixed, starts, edges, downs = [], [], [], []
    turned_gated, d_gates, d_raws, small_scan = [], [], [], []

    def project_step(at, wait=()):
        gate, raw, flat = project_tokens(normed_near, normed_far, at, weight, inner, wait)
        gates.append(gate)
        raws.append(raw.reshape(1, length, raw.shape[-1]))
        turned_normed.append(flat)

    def forward_step(at, wait=()):
        got = scan_forward(half_at, raws[at], 0, *params, wait=wait)
        mixed.append(got[0].reshape(natural + (inner,)))
        starts.append(got[1])
        edges.append(got[2])

    def stats_step(at, wait=()):
        down, own = gate_stats(
            grad_near, at, grad_far, at, w_out, mixed[at], gates[at], gain_own, wait
        )
        downs.append(down)
        return own

    def back_step(at, sums, wait=()):
        flat, d_mixed, d_gate, out, gain = gate_back(
            mixed[at], gates[at], downs[at], sums, gain_own, w_out, wait
        )
        turned_gated.append(flat)
        d_gates.append(d_gate)
        return d_mixed, out, gain

    def scan_step(at, d_mixed, wait=()):
        d_mixed = d_mixed.reshape(1, length, inner)
        d_raw, *small = scan_backward(
            half_at, raws[at], 0, d_mixed, starts[at], edges[at], *params, wait=wait
        )
        d_raws.append(d_raw[0])
        small_scan.append(small)

    def norm_step(at, wait=()):
        d_raw = d_raws[at].reshape(natural + (d_raws[at].shape[-1],))
        return norm_part(d_gates[at], d_raw, normed_near, normed_far, at, weight, wait)

    def owned_parts(part):
        blocks = part.reshape(lay.parts, lay.wsh, in_rows, part.shape[1])
        kept = pick(blocks, lay.wplace, 1)
        away = [pick(blocks, (lay.wplace + d) % lay.wsh, 1) for d in range(1, lay.wsh)]
        return kept, [lay.wsh_shift(a, d + 1) for d, a in enumerate(away)]

    def to_owners(kept):
        return lax.all_to_all(kept, ALL, split_axis=0, concat_axis=0, tiled=True)

    def add_owned(kept, came):
        total = kept.astype(F32)
        for part in came:
            total = total + part.astype(F32)
        return total.astype(BF16)

    cross, first_pairs, second_pairs = [], [], []
    for half in range(2):
        for chip in range(lay.chips):
            source = (half * lay.chips + chip) * 2 + half
            peer = ((1 - half) * lay.chips + chip) * 2 + half
            head_block = half * lay.chips + chip
            cross.append((peer, source))
            first_pairs.append((source, 2 * head_block))
            second_pairs.append((source, 2 * head_block + 1))

    def out_split(values):
        values = values.reshape(2, lay.wsh, out_rows, model)
        kept = pick(values, lay.wplace, 1)
        away = [pick(values, (lay.wplace + d) % lay.wsh, 1) for d in range(1, lay.wsh)]
        return kept, [lay.wsh_shift(a, d + 1) for d, a in enumerate(away)]

    def over_groups(values):
        parts = []
        for bits in range(lay.wsh):
            moved = values
            if bits:
                pairs = [(i, i ^ bits) for i in range(lay.wsh)]
                moved = lax.ppermute(values, "wsh", pairs)
            both = []
            for i in range(lay.wsh):
                both += [(i, lay.wsh + (i ^ bits)), (lay.wsh + i, i ^ bits)]
            parts += [moved, lax.ppermute(values, ("half", "wsh"), both)]
        return parts

    project_step(0)
    forward_step(0)
    project_step(1, (edges[0],))
    forward_step(1)
    out_pieces, mixed[1] = join(out_pieces, mixed[1])
    w_out = own_rows(*out_pieces)
    own = stats_step(0)
    parts = team_parts(own, lay)
    own1 = stats_step(1, (own,))
    sums = add_all(parts)
    d_mixed0, out, gain0 = back_step(0, sums, (own1,))
    parts, out, gain0 = join(team_parts(own1, lay), out, gain0)
    out0 = team_sum(out)
    d_mixed1, out, gain1 = back_step(1, add_all(parts))
    out1 = team_sum(out)
    flat_gates = [d.reshape(length, inner) for d in d_gates]
    gate_grad = row_grad(
        [(turned_normed[0], flat_gates[0]), (turned_normed[1], flat_gates[1])], BF16
    )
    gate_kept, gate_came = owned_parts(gate_grad)
    scan_step(0, d_mixed0, (gate_kept,))
    gate_came, d_raws[0] = join(gate_came, d_raws[0])
    by_gate = to_owners(add_owned(gate_kept, gate_came))
    out_grad = out_grad_part(turned_gated, grad_near, grad_far, wait=(d_raws[0],))
    out_kept, out_came = out_split(out_grad)
    part, norm_gain0 = norm_step(0, (out_kept,))
    d_mixed1, part = join(d_mixed1, part)
    norm0 = team_sum(part)
    sum0 = two_halves(out0, lay)
    scan_step(1, d_mixed1)
    out_came, d_raws[1] = join(out_came, d_raws[1])
    out_kept = add_owned(out_kept, out_came)
    out_came = lax.ppermute(out_kept, ALL, cross)
    part, norm_gain1 = norm_step(1)
    scan_grad = row_grad(
        [(turned_normed[0], d_raws[0]), (turned_normed[1], d_raws[1])], BF16, wait=(norm_gain1,)
    )
    scan_kept, scan_came = owned_parts(scan_grad)
    by_gate, out_came, sum0, scan_kept, part = join(by_gate, out_came, sum0, scan_kept, part)
    norm1 = team_sum(part)
    out_held = (out_kept.astype(F32) + out_came.astype(F32)).astype(BF16)
    out_first = lax.ppermute(out_held[0], ALL, first_pairs)
    out_second = lax.ppermute(out_held[1], ALL, second_pairs)
    small = over_groups(own_small(norm_gain1))
    scan_came, sum1, norm0, small = join(
        scan_came, two_halves(out1, lay), two_halves(norm0, lay), small
    )
    by_scan = to_owners(add_owned(scan_kept, scan_came))
    small = team_parts(pack_small(add_all(small)), lay)
    by_scan, small = join(by_scan, small)
    norm1 = two_halves(norm1, lay)
    small = add_all(small)
    out_proj_grad = out_first.astype(F32) + out_second.astype(F32)

    def whole_place(first, second):
        mine = jnp.stack([first[0], second[0]], 0)
        other = jnp.stack([first[1], second[1]], 0)
        return both_halves(mine, other, lay)

    block_out = (hidden_wide + whole_place(sum0, sum1).astype(F32)).astype(BF16)

    def hidden_step():
        d_scaled = whole_place(norm0, norm1).astype(F32) * norm_gain
        inward = jnp.mean(d_scaled * hidden_wide, axis=-1, keepdims=True)
        return (
            cotangent.astype(F32)
            + norm_scale * d_scaled
            - hidden_wide * (norm_scale * norm_scale * norm_scale * inward)
        )

    hidden_grad = hidden_step()

    order = [(b % lay.chips) * 2 + b // lay.chips for b in range(team)]

    def by_member_parts(parts):
        return parts.reshape(2, team, in_rows, parts.shape[-1])

    in_proj_grad = owned_rows(order, by_member_parts(by_gate), by_member_parts(by_scan))
    ngain_all, conv_all, cbias_all, shift_all, rate_all, skip_all, ggain_all = unpack_small(small)
    return (
        block_out,
        hidden_grad,
        ngain_all,
        in_proj_grad,
        conv_all,
        cbias_all,
        shift_all,
        rate_all,
        skip_all,
        ggain_all,
        out_proj_grad,
    )


def solution(mesh):
    parts, wsh = mesh.devices.shape
    fine = Mesh(mesh.devices.reshape(2, parts // 4, 2, wsh), ("half", "chip", "core", "wsh"))
    by_token = P("wsh", ALL, None)
    by_row = P("wsh", None)
    owned = P(ALL + ("wsh",), None)
    whole = P()
    return jax.shard_map(
        shards,
        mesh=fine,
        in_specs=(by_token, by_token, whole, by_row) + (whole,) * 6 + (by_row,),
        out_specs=(by_token, by_token, whole, owned) + (whole,) * 6 + (owned,),
        check_vma=False,
    )
```
